32 devices in a mesh: dp: 4 (over y, x), expert: 8 (over z, core).
Axes of the slice: x: 2, y: 2, z: 4, core: 2. Of those that a mesh axis runs over, the one named last changes fastest.
Arguments:
- tokens: bfloat16 [768, 4096], P('expert', 'dp'), may hold values from -6 to 6
- expert_ids: int32 [768, 8], P('expert'), may hold values from 0 to 7, as said below
- gate_probs: float32 [768, 8], P('expert'), may hold values from 0.05 to 1
- gate_weight: bfloat16 [8, 4096, 768], P('expert', 'dp'), may hold values from -0.09375 to 0.09375
- up_weight: bfloat16 [8, 4096, 768], P('expert', 'dp'), may hold values from -0.09375 to 0.09375
- down_weight: bfloat16 [8, 768, 4096], P('expert', None, 'dp'), may hold values from -0.21875 to 0.21875
- out_grad: bfloat16 [768, 4096], P('expert', 'dp'), may hold values from -6 to 6
Outputs:
- layer_out: bfloat16 [768, 4096], P('expert', 'dp')
- token_grad: bfloat16 [768, 4096], P('expert', 'dp')
- gate_grad: bfloat16 [8, 4096, 768], P('expert', 'dp')
- up_grad: bfloat16 [8, 4096, 768], P('expert', 'dp')
- down_grad: bfloat16 [8, 768, 4096], P('expert', None, 'dp')
The draws below stay inside these ranges and needn't reach their ends.
Inputs may be any that keep to these rules, and one draw needn't show every extreme that they name: `expert_ids`: each row names 8 different experts. Among the 96 rows of one device (aligned blocks) no expert is named by more than 96 rows, and some expert is named by exactly 96 rows in every such block.
All inputs are finite; a program needn't handle non-finite values.
Results may differ from the reference program's by a relative error of at most 0.018.
Values may be sent and summed in bfloat16 or wider, within the bound.
A program may use at most 64 MiB of HBM per device.

```python
import math
import jax
import jax.numpy as jnp
from jax import lax

D = 4096
TOPK = 8
FF = 768
TOK_DEV = 96
EXPERTS = 8
TOKENS = 768
MOST = 96
N_DP = 4


def draw_expert_ids(key, part):
    key = jax.random.fold_in(key, 7)
    blocks = TOKENS // TOK_DEV
    unit_count = EXPERTS * MOST
    needed = TOK_DEV * TOPK
    popularity = jax.random.randint(jax.random.fold_in(key, 1), (EXPERTS,), 0, 4)
    favourite = jax.random.randint(jax.random.fold_in(key, 2), (), 0, EXPERTS)
    expert_of_unit = jnp.arange(unit_count, dtype=jnp.int32) // MOST

    def one_block(block_key):
        noise_key, order_key, column_key = jax.random.split(block_key, 3)
        noise_val = jax.random.randint(noise_key, (unit_count,), 0, 2048)
        priority = noise_val + 400 * popularity[expert_of_unit]
        priority = jnp.where(expert_of_unit == favourite, 8192, priority)
        ranked = priority * unit_count + jnp.arange(unit_count, dtype=jnp.int32)
        chosen = jnp.argsort(-ranked)[:needed]
        picked = jnp.sort(expert_of_unit[chosen])
        layout = picked.reshape(TOPK, TOK_DEV).T
        shuffle = jax.random.randint(column_key, (TOK_DEV, TOPK), 0, 1024) * TOPK + jnp.arange(TOPK, dtype=jnp.int32)[None, :]
        layout = jnp.take_along_axis(layout, jnp.argsort(shuffle, axis=1), axis=1)
        return layout[jax.random.permutation(order_key, TOK_DEV)]
    block_keys = jax.random.split(jax.random.fold_in(key, 3), blocks)
    return jax.vmap(one_block)(block_keys).reshape(TOKENS, TOPK).astype(jnp.int32)


def level_of(own_key, shape, pieces, least, high):
    def one(axis_at, parts):
        draws = jax.random.uniform(jax.random.fold_in(jax.random.fold_in(own_key, 6), axis_at), (parts,), jnp.float32, least / len(pieces), high / len(pieces))
        return jnp.repeat(jnp.exp(draws), shape[axis_at] // parts).reshape((-1,) + (1,) * (len(shape) - axis_at - 1))

    loudness = one(*pieces[0])
    for cut in pieces[1:]:
        loudness = loudness * one(*cut)
    return loudness


def bell_draw(stream_key, dims, scale, reach, cuts=(), held_as=jnp.bfloat16):
    values = jax.random.normal(stream_key, dims, jnp.float32) * scale
    if len(cuts) > 0:
        values = level_of(stream_key, dims, cuts, -0.22, 0.18) * values
    return jnp.clip(values, min=-reach, max=reach).astype(held_as)


def setup_inputs(seed: int = 0) -> dict:
    keys = jax.random.split(jax.random.key(seed), 8)
    return {
        "tokens": bell_draw(keys[0], (TOKENS, D), 1.0, 6.0, ((0, 8), (1, 4))),
        "expert_ids": draw_expert_ids(jax.random.fold_in(keys[7], 71), 0),
        "gate_probs": jnp.clip(jnp.exp(math.log(1.0) - 2.9957323 * jax.random.uniform(keys[2], (TOKENS, TOPK), jnp.float32) ** level_of(keys[2], (TOKENS, TOPK), ((0, 8),), -0.2, 0.2)), 0.05, 1.0),
        "gate_weight": bell_draw(keys[3], (EXPERTS, D, FF), D ** -0.5, 0.09375, ((0, 8), (1, 4))),
        "up_weight": bell_draw(keys[4], (EXPERTS, D, FF), D ** -0.5, 0.09375, ((0, 8), (1, 4))),
        "down_weight": bell_draw(keys[5], (EXPERTS, FF, D), FF ** -0.5, 0.21875, ((0, 8), (2, 4))),
        "out_grad": bell_draw(keys[6], (TOKENS, D), 1.0, 6.0, ((0, 8), (1, 4))),
    }


def rounded(values):
    return lax.optimization_barrier(values.astype(jnp.bfloat16)).astype(jnp.float32)


def reference(tokens, expert_ids, gate_probs, gate_weight, up_weight, down_weight, out_grad):
    groups = TOKENS // TOK_DEV
    slot_count = groups * MOST
    pair_count = TOK_DEV * TOPK
    quarter = D // N_DP
    weights = gate_probs / jnp.sum(gate_probs, axis=1, keepdims=True)
    route_ids = expert_ids.reshape(groups, pair_count)
    onehot = (route_ids[:, :, None] == jnp.arange(EXPERTS, dtype=jnp.int32)[None, None, :]).astype(jnp.int32)
    position = jnp.sum((jnp.cumsum(onehot, axis=1) - onehot) * onehot, axis=2)
    source = jnp.arange(groups, dtype=jnp.int32)[:, None]
    slot_place = route_ids * slot_count + source * MOST + position
    pair_index = jnp.arange(TOKENS * TOPK, dtype=jnp.int32)
    slot_table = jnp.full((EXPERTS * slot_count,), TOKENS * TOPK, jnp.int32)
    slot_table = slot_table.at[slot_place.reshape(-1)].set(pair_index).reshape(EXPERTS, slot_count)
    token_rows = jnp.concatenate([tokens, jnp.zeros((1, D), jnp.bfloat16)], axis=0)
    grad_rows = jnp.concatenate([out_grad, jnp.zeros((1, D), jnp.bfloat16)], axis=0)
    pair_weights = jnp.concatenate([weights.reshape(-1), jnp.zeros((1,), jnp.float32)], axis=0)

    def per_expert(state, inputs):
        out_acc, grad_acc = state
        w_gate, w_up, w_down, entries = inputs
        token_of = entries // TOPK
        token_block = token_rows[token_of]
        pair_weight = pair_weights[entries]
        gate_pre = sum(rounded(jnp.dot(token_block[:, quarter_index * quarter:(quarter_index + 1) * quarter], w_gate[quarter_index * quarter:(quarter_index + 1) * quarter], preferred_element_type=jnp.float32)) for quarter_index in range(N_DP))
        up_pre = sum(rounded(jnp.dot(token_block[:, quarter_index * quarter:(quarter_index + 1) * quarter], w_up[quarter_index * quarter:(quarter_index + 1) * quarter], preferred_element_type=jnp.float32)) for quarter_index in range(N_DP))
        hidden = (jax.nn.silu(gate_pre) * up_pre).astype(jnp.bfloat16)
        expert_out = jnp.dot(hidden, w_down, preferred_element_type=jnp.float32).astype(jnp.bfloat16)
        out_acc = out_acc.at[token_of].add(pair_weight[:, None] * expert_out.astype(jnp.float32))
        pair_grad = (pair_weight[:, None] * grad_rows[token_of].astype(jnp.float32)).astype(jnp.bfloat16)
        hidden_grad = sum(rounded(jnp.dot(pair_grad[:, quarter_index * quarter:(quarter_index + 1) * quarter], w_down[:, quarter_index * quarter:(quarter_index + 1) * quarter].T, preferred_element_type=jnp.float32)) for quarter_index in range(N_DP))
        sigmoid_gate = jax.nn.sigmoid(gate_pre)
        gate_pre_grad = (hidden_grad * up_pre * sigmoid_gate * (1.0 + gate_pre * (1.0 - sigmoid_gate))).astype(jnp.bfloat16)
        up_pre_grad = (hidden_grad * jax.nn.silu(gate_pre)).astype(jnp.bfloat16)
        pair_token = (jnp.dot(gate_pre_grad, w_gate.T, preferred_element_type=jnp.float32) + jnp.dot(up_pre_grad, w_up.T, preferred_element_type=jnp.float32)).astype(jnp.bfloat16)
        grad_acc = grad_acc.at[token_of].add(pair_token.astype(jnp.float32))
        gate_grad = jnp.dot(token_block.T, gate_pre_grad, preferred_element_type=jnp.float32).astype(jnp.bfloat16)
        up_grad = jnp.dot(token_block.T, up_pre_grad, preferred_element_type=jnp.float32).astype(jnp.bfloat16)
        down_grad = jnp.dot(hidden.T, pair_grad, preferred_element_type=jnp.float32).astype(jnp.bfloat16)
        return (out_acc, grad_acc), (gate_grad, up_grad, down_grad)

    start_state = (jnp.zeros((TOKENS + 1, D), jnp.float32), jnp.zeros((TOKENS + 1, D), jnp.float32))
    final_state, grads = lax.scan(per_expert, start_state, (gate_weight, up_weight, down_weight, slot_table))
    out_acc, grad_acc = final_state
    gate_grad, up_grad, down_grad = grads
    return (out_acc[:TOKENS].astype(jnp.bfloat16), grad_acc[:TOKENS].astype(jnp.bfloat16), gate_grad, up_grad, down_grad)
```

```python
import jax
import jax.numpy as jnp
from jax import lax
from jax.sharding import PartitionSpec as P


def rounded(values):
    return lax.optimization_barrier(values.astype(jnp.bfloat16)).astype(jnp.float32)


def contract_last(first_op, second_op):
    return lax.dot_general(
        first_op, second_op, (((1,), (1,)), ((), ())), preferred_element_type=jnp.float32
    )


def contract_rows(first_op, second_op):
    return lax.dot_general(
        first_op, second_op, (((0,), (0,)), ((), ())), preferred_element_type=jnp.float32
    )


def swish_grads(grad_in, gate_pre, up_pre):
    sigmoid_gate = jax.nn.sigmoid(gate_pre)
    gate_pre_grad = (
        grad_in * up_pre * sigmoid_gate * (1.0 + gate_pre * (1.0 - sigmoid_gate))
    ).astype(jnp.bfloat16)
    up_pre_grad = (grad_in * jax.nn.silu(gate_pre)).astype(jnp.bfloat16)
    return (gate_pre_grad, up_pre_grad)


def send_back(values):
    return lax.all_to_all(values, "expert", split_axis=0, concat_axis=0, tiled=True)


def sparse_body(tokens, expert_ids, gate_probs, gate_weight, up_weight, down_weight, out_grad):
    tok_rows, width_part = tokens.shape
    top_count = expert_ids.shape[1]
    groups = lax.axis_size("expert")
    capacity = min(tok_rows, 4 * tok_rows * top_count // (3 * groups))
    slot_count = groups * capacity
    pair_count = tok_rows * top_count
    hidden_units = gate_weight.shape[2]
    w_gate = gate_weight[0]
    w_up = up_weight[0]
    w_down = down_weight[0]
    weights = gate_probs / jnp.sum(gate_probs, axis=1, keepdims=True)
    flat_ids = expert_ids.reshape(pair_count)
    onehot = (flat_ids[:, None] == jnp.arange(groups, dtype=jnp.int32)[None, :]).astype(jnp.int32)
    earlier = jnp.cumsum(onehot, axis=0) - onehot
    position = jnp.sum(earlier * onehot, axis=1)
    slot_of_pair = flat_ids * capacity + position
    pair_of_slot = (
        jnp.full((slot_count,), pair_count, jnp.int32)
        .at[slot_of_pair]
        .set(jnp.arange(pair_count, dtype=jnp.int32))
    )
    token_of_slot = pair_of_slot // top_count
    zero_row = jnp.zeros((1, width_part), jnp.bfloat16)
    send_rows = jnp.concatenate([tokens, zero_row], axis=0)[token_of_slot].reshape(
        groups, capacity, width_part
    )

    def run_blocks(step_fn, initial):
        return step_fn(0, slot_count, initial)

    expert_rows = lax.all_to_all(
        send_rows, "expert", split_axis=0, concat_axis=0, tiled=True
    ).reshape(slot_count, width_part)

    def gate_up_step(offset, length, current):
        gate_acc = rounded(jnp.dot(expert_rows, w_gate, preferred_element_type=jnp.float32))
        up_acc = rounded(jnp.dot(expert_rows, w_up, preferred_element_type=jnp.float32))
        return (gate_acc, up_acc)

    zero_hidden = jnp.zeros((slot_count, hidden_units), jnp.float32)
    gate_part, up_part = run_blocks(gate_up_step, (zero_hidden, zero_hidden))
    gate_pre, up_pre = (
        lax.psum(gate_part.astype(jnp.bfloat16), "dp").astype(jnp.float32),
        lax.psum(up_part.astype(jnp.bfloat16), "dp").astype(jnp.float32),
    )
    hidden = (jax.nn.silu(gate_pre) * up_pre).astype(jnp.bfloat16)

    def down_step(offset, length, current):
        result_rows = jnp.dot(hidden, w_down, preferred_element_type=jnp.float32).astype(
            jnp.bfloat16
        )
        return result_rows

    expert_out = run_blocks(down_step, jnp.zeros((slot_count, width_part), jnp.bfloat16))
    returned = send_back(expert_out.reshape(groups, capacity, width_part)).reshape(
        slot_count, width_part
    )
    pair_out = returned[slot_of_pair].reshape(tok_rows, top_count, width_part)
    layer_out = jnp.sum(weights[:, :, None] * pair_out.astype(jnp.float32), axis=1).astype(
        jnp.bfloat16
    )
    pair_grad = (
        (weights[:, :, None] * out_grad[:, None, :].astype(jnp.float32))
        .astype(jnp.bfloat16)
        .reshape(pair_count, width_part)
    )
    send_grads = jnp.concatenate([pair_grad, zero_row], axis=0)[pair_of_slot].reshape(
        groups, capacity, width_part
    )
    grad_rows = lax.all_to_all(
        send_grads, "expert", split_axis=0, concat_axis=0, tiled=True
    ).reshape(slot_count, width_part)

    def hidden_grad_step(offset, length, current):
        hidden_acc = rounded(contract_last(grad_rows, w_down))
        down_acc = contract_rows(hidden, grad_rows)
        return (hidden_acc, down_acc)

    hidden_grad_part, down_total = run_blocks(
        hidden_grad_step, (zero_hidden, jnp.zeros((hidden_units, width_part), jnp.float32))
    )
    hidden_grad = lax.psum(hidden_grad_part.astype(jnp.bfloat16), "dp").astype(jnp.float32)
    gate_pre_grad, up_pre_grad = swish_grads(hidden_grad, gate_pre, up_pre)

    def token_step(offset, length, current):
        pair_token = (
            contract_last(gate_pre_grad, w_gate) + contract_last(up_pre_grad, w_up)
        ).astype(jnp.bfloat16)
        gate_acc = contract_rows(expert_rows, gate_pre_grad)
        up_acc = contract_rows(expert_rows, up_pre_grad)
        return (pair_token, gate_acc, up_acc)

    zero_weight = jnp.zeros((width_part, hidden_units), jnp.float32)
    token_part, gate_total, up_total = run_blocks(
        token_step, (jnp.zeros((slot_count, width_part), jnp.bfloat16), zero_weight, zero_weight)
    )
    returned_grad = send_back(token_part.reshape(groups, capacity, width_part)).reshape(
        slot_count, width_part
    )
    pair_token_grad = returned_grad[slot_of_pair].reshape(tok_rows, top_count, width_part)
    token_grad = jnp.sum(pair_token_grad.astype(jnp.float32), axis=1).astype(jnp.bfloat16)
    return (
        layer_out,
        token_grad,
        gate_total.astype(jnp.bfloat16)[None],
        up_total.astype(jnp.bfloat16)[None],
        down_total.astype(jnp.bfloat16)[None],
    )


def dense_body(tokens, expert_ids, gate_probs, gate_weight, up_weight, down_weight, out_grad):
    groups = lax.axis_size("expert")
    me = lax.axis_index("expert")
    w_gate = gate_weight[0]
    w_up = up_weight[0]
    w_down = down_weight[0]
    weights = gate_probs / jnp.sum(gate_probs, axis=1, keepdims=True)
    named = expert_ids[:, :, None] == jnp.arange(groups, dtype=jnp.int32)[None, None, :]
    by_expert = jnp.sum(jnp.where(named, weights[:, :, None], 0.0), axis=1)
    all_weights = lax.all_gather(by_expert, "expert", axis=0, tiled=True)
    mine = jnp.arange(groups, dtype=jnp.int32)[None, :] == me
    weight = jnp.sum(jnp.where(mine, all_weights, 0.0), axis=1, keepdims=True)
    rows = lax.all_gather(tokens, "expert", axis=0, tiled=True)
    grads = lax.all_gather(out_grad, "expert", axis=0, tiled=True)
    pair_grad = (weight * grads.astype(jnp.float32)).astype(jnp.bfloat16)

    def total(values):
        return lax.psum(values.astype(jnp.bfloat16), "dp").astype(jnp.float32)

    gate_pre = total(jnp.dot(rows, w_gate, preferred_element_type=jnp.float32))
    up_pre = total(jnp.dot(rows, w_up, preferred_element_type=jnp.float32))
    hidden_grad = total(contract_last(pair_grad, w_down))
    hidden = (jax.nn.silu(gate_pre) * up_pre).astype(jnp.bfloat16)
    expert_out = jnp.dot(hidden, w_down, preferred_element_type=jnp.float32)
    layer_out = lax.psum_scatter(
        (weight * expert_out).astype(jnp.bfloat16), "expert", scatter_dimension=0, tiled=True
    )
    gate_pre_grad, up_pre_grad = swish_grads(hidden_grad, gate_pre, up_pre)
    pair_token = contract_last(gate_pre_grad, w_gate) + contract_last(up_pre_grad, w_up)
    token_grad = lax.psum_scatter(
        pair_token.astype(jnp.bfloat16), "expert", scatter_dimension=0, tiled=True
    )
    return (
        layer_out,
        token_grad,
        contract_rows(rows, gate_pre_grad).astype(jnp.bfloat16)[None],
        contract_rows(rows, up_pre_grad).astype(jnp.bfloat16)[None],
        contract_rows(hidden, pair_grad).astype(jnp.bfloat16)[None],
    )


def body(tokens, expert_ids, *rest):
    if expert_ids.shape[1] == lax.axis_size("expert"):
        return dense_body(tokens, expert_ids, *rest)
    return sparse_body(tokens, expert_ids, *rest)


def solution(mesh):
    placed = (
        P("expert", "dp"),
        P("expert", None),
        P("expert", None),
        P("expert", "dp", None),
        P("expert", "dp", None),
        P("expert", None, "dp"),
        P("expert", "dp"),
    )
    return jax.shard_map(
        body,
        mesh=mesh,
        in_specs=placed,
        out_specs=(
            P("expert", "dp"),
            P("expert", "dp"),
            P("expert", "dp", None),
            P("expert", "dp", None),
            P("expert", None, "dp"),
        ),
        check_vma=False,
    )
```

```python
import jax
import jax.numpy as jnp
from jax import lax
from jax.experimental import pallas as pl
from jax.experimental.pallas import tpu as pltpu
from jax.sharding import PartitionSpec as P


def rounded(values):
    return lax.optimization_barrier(values.astype(jnp.bfloat16)).astype(jnp.float32)


def contract_last(first_op, second_op):
    return lax.dot_general(
        first_op, second_op, (((1,), (1,)), ((), ())), preferred_element_type=jnp.float32
    )


def contract_rows(first_op, second_op):
    return lax.dot_general(
        first_op, second_op, (((0,), (0,)), ((), ())), preferred_element_type=jnp.float32
    )


def swish_grads(grad_in, gate_pre, up_pre):
    sigmoid_gate = jax.nn.sigmoid(gate_pre)
    gate_pre_grad = (
        grad_in * up_pre * sigmoid_gate * (1.0 + gate_pre * (1.0 - sigmoid_gate))
    ).astype(jnp.bfloat16)
    up_pre_grad = (grad_in * jax.nn.silu(gate_pre)).astype(jnp.bfloat16)
    return (gate_pre_grad, up_pre_grad)


def send_back(values):
    return lax.all_to_all(values, "expert", split_axis=0, concat_axis=0, tiled=True)


def sparse_body(tokens, expert_ids, gate_probs, gate_weight, up_weight, down_weight, out_grad):
    tok_rows, width_part = tokens.shape
    top_count = expert_ids.shape[1]
    groups = lax.axis_size("expert")
    capacity = min(tok_rows, 4 * tok_rows * top_count // (3 * groups))
    slot_count = groups * capacity
    pair_count = tok_rows * top_count
    hidden_units = gate_weight.shape[2]
    w_gate = gate_weight[0]
    w_up = up_weight[0]
    w_down = down_weight[0]
    weights = gate_probs / jnp.sum(gate_probs, axis=1, keepdims=True)
    flat_ids = expert_ids.reshape(pair_count)
    onehot = (flat_ids[:, None] == jnp.arange(groups, dtype=jnp.int32)[None, :]).astype(jnp.int32)
    earlier = jnp.cumsum(onehot, axis=0) - onehot
    position = jnp.sum(earlier * onehot, axis=1)
    slot_of_pair = flat_ids * capacity + position
    pair_of_slot = (
        jnp.full((slot_count,), pair_count, jnp.int32)
        .at[slot_of_pair]
        .set(jnp.arange(pair_count, dtype=jnp.int32))
    )
    token_of_slot = pair_of_slot // top_count
    zero_row = jnp.zeros((1, width_part), jnp.bfloat16)
    send_rows = jnp.concatenate([tokens, zero_row], axis=0)[token_of_slot].reshape(
        groups, capacity, width_part
    )

    def run_blocks(step_fn, initial):
        return step_fn(0, slot_count, initial)

    expert_rows = lax.all_to_all(
        send_rows, "expert", split_axis=0, concat_axis=0, tiled=True
    ).reshape(slot_count, width_part)

    def gate_up_step(offset, length, current):
        gate_acc = rounded(jnp.dot(expert_rows, w_gate, preferred_element_type=jnp.float32))
        up_acc = rounded(jnp.dot(expert_rows, w_up, preferred_element_type=jnp.float32))
        return (gate_acc, up_acc)

    zero_hidden = jnp.zeros((slot_count, hidden_units), jnp.float32)
    gate_part, up_part = run_blocks(gate_up_step, (zero_hidden, zero_hidden))
    gate_pre, up_pre = (
        lax.psum(gate_part.astype(jnp.bfloat16), "dp").astype(jnp.float32),
        lax.psum(up_part.astype(jnp.bfloat16), "dp").astype(jnp.float32),
    )
    hidden = (jax.nn.silu(gate_pre) * up_pre).astype(jnp.bfloat16)

    def down_step(offset, length, current):
        result_rows = jnp.dot(hidden, w_down, preferred_element_type=jnp.float32).astype(
            jnp.bfloat16
        )
        return result_rows

    expert_out = run_blocks(down_step, jnp.zeros((slot_count, width_part), jnp.bfloat16))
    returned = send_back(expert_out.reshape(groups, capacity, width_part)).reshape(
        slot_count, width_part
    )
    pair_out = returned[slot_of_pair].reshape(tok_rows, top_count, width_part)
    layer_out = jnp.sum(weights[:, :, None] * pair_out.astype(jnp.float32), axis=1).astype(
        jnp.bfloat16
    )
    pair_grad = (
        (weights[:, :, None] * out_grad[:, None, :].astype(jnp.float32))
        .astype(jnp.bfloat16)
        .reshape(pair_count, width_part)
    )
    send_grads = jnp.concatenate([pair_grad, zero_row], axis=0)[pair_of_slot].reshape(
        groups, capacity, width_part
    )
    grad_rows = lax.all_to_all(
        send_grads, "expert", split_axis=0, concat_axis=0, tiled=True
    ).reshape(slot_count, width_part)

    def hidden_grad_step(offset, length, current):
        hidden_acc = rounded(contract_last(grad_rows, w_down))
        down_acc = contract_rows(hidden, grad_rows)
        return (hidden_acc, down_acc)

    hidden_grad_part, down_total = run_blocks(
        hidden_grad_step, (zero_hidden, jnp.zeros((hidden_units, width_part), jnp.float32))
    )
    hidden_grad = lax.psum(hidden_grad_part.astype(jnp.bfloat16), "dp").astype(jnp.float32)
    gate_pre_grad, up_pre_grad = swish_grads(hidden_grad, gate_pre, up_pre)

    def token_step(offset, length, current):
        pair_token = (
            contract_last(gate_pre_grad, w_gate) + contract_last(up_pre_grad, w_up)
        ).astype(jnp.bfloat16)
        gate_acc = contract_rows(expert_rows, gate_pre_grad)
        up_acc = contract_rows(expert_rows, up_pre_grad)
        return (pair_token, gate_acc, up_acc)

    zero_weight = jnp.zeros((width_part, hidden_units), jnp.float32)
    token_part, gate_total, up_total = run_blocks(
        token_step, (jnp.zeros((slot_count, width_part), jnp.bfloat16), zero_weight, zero_weight)
    )
    returned_grad = send_back(token_part.reshape(groups, capacity, width_part)).reshape(
        slot_count, width_part
    )
    pair_token_grad = returned_grad[slot_of_pair].reshape(tok_rows, top_count, width_part)
    token_grad = jnp.sum(pair_token_grad.astype(jnp.float32), axis=1).astype(jnp.bfloat16)
    return (
        layer_out,
        token_grad,
        gate_total.astype(jnp.bfloat16)[None],
        up_total.astype(jnp.bfloat16)[None],
        down_total.astype(jnp.bfloat16)[None],
    )


def dense_body(tokens, expert_ids, gate_probs, gate_weight, up_weight, down_weight, out_grad):
    groups = lax.axis_size("expert")
    me = lax.axis_index("expert")
    w_gate = gate_weight[0]
    w_up = up_weight[0]
    w_down = down_weight[0]
    weights = gate_probs / jnp.sum(gate_probs, axis=1, keepdims=True)
    named = expert_ids[:, :, None] == jnp.arange(groups, dtype=jnp.int32)[None, None, :]
    by_expert = jnp.sum(jnp.where(named, weights[:, :, None], 0.0), axis=1)
    all_weights = lax.all_gather(by_expert, "expert", axis=0, tiled=True)
    mine = jnp.arange(groups, dtype=jnp.int32)[None, :] == me
    weight = jnp.sum(jnp.where(mine, all_weights, 0.0), axis=1, keepdims=True)
    rows = lax.all_gather(tokens, "expert", axis=0, tiled=True)
    grads = lax.all_gather(out_grad, "expert", axis=0, tiled=True)
    pair_grad = (weight * grads.astype(jnp.float32)).astype(jnp.bfloat16)

    def total(values):
        return lax.psum(values.astype(jnp.bfloat16), "dp").astype(jnp.float32)

    gate_pre = total(jnp.dot(rows, w_gate, preferred_element_type=jnp.float32))
    up_pre = total(jnp.dot(rows, w_up, preferred_element_type=jnp.float32))
    hidden_grad = total(contract_last(pair_grad, w_down))
    hidden = (jax.nn.silu(gate_pre) * up_pre).astype(jnp.bfloat16)
    expert_out = jnp.dot(hidden, w_down, preferred_element_type=jnp.float32)
    layer_out = lax.psum_scatter(
        (weight * expert_out).astype(jnp.bfloat16), "expert", scatter_dimension=0, tiled=True
    )
    gate_pre_grad, up_pre_grad = swish_grads(hidden_grad, gate_pre, up_pre)
    pair_token = contract_last(gate_pre_grad, w_gate) + contract_last(up_pre_grad, w_up)
    token_grad = lax.psum_scatter(
        pair_token.astype(jnp.bfloat16), "expert", scatter_dimension=0, tiled=True
    )
    return (
        layer_out,
        token_grad,
        contract_rows(rows, gate_pre_grad).astype(jnp.bfloat16)[None],
        contract_rows(rows, up_pre_grad).astype(jnp.bfloat16)[None],
        contract_rows(hidden, pair_grad).astype(jnp.bfloat16)[None],
    )


TILE = 256
BLOCKS = 4
PEERS = 4
MESH = pl.DeviceIdType.MESH


def layer_kernel(
    tok_ref, grad_ref, wt_ref, wg_ref, wu_ref, wd_ref,
    out_ref, tgrad_ref, gg_ref, ug_ref, dg_ref,
    tok_all, grd_all, wt_all, wcol, pg_all,
    gu_part, gu_in, hg_part, hg_in, gpre, upre, hid_all, dgu_all,
    eo, eo_in, eo_sum, eo_z, tg, tg_in, tg_sum, tg_z,
    tok_s, tok_r, grd_s, grd_r, tokf_s, grdf_s, wt_s, wt_r,
    gu_s, gu_r, hg_s, hg_r, hid_s, hid_r, dgu_s, dgu_r,
    eo_s, eo_r, eoz_s, eoz_r, tg_s, tg_r, tgz_s, tgz_r,
):
    dp = lax.axis_index("dp")
    ex = lax.axis_index("expert")
    z = ex // 2
    c = ex % 2
    oc = 1 - c
    rows, width = tok_ref.shape
    units = wg_ref.shape[1]
    share = gu_part.shape[2]
    both = 2 * rows
    bf16 = jnp.bfloat16
    f32 = jnp.float32

    def block_at(step):
        return ((z // 2 + step // 2) % 2) * 2 + (z + step) % 2

    def peer_at(k):
        return (dp + k) % PEERS

    def remote(src, dst, send, recv, to_dp, to_ex):
        return pltpu.make_async_remote_copy(
            src_ref=src, dst_ref=dst, send_sem=send, recv_sem=recv,
            device_id=(to_dp, to_ex), device_id_type=MESH,
        )

    barrier = pltpu.get_barrier_semaphore()
    for k in range(1, 8):
        pl.semaphore_signal(barrier, inc=1, device_id=(dp, (ex + k) % 8), device_id_type=MESH)
    for k in range(1, PEERS):
        pl.semaphore_signal(barrier, inc=1, device_id=(peer_at(k), ex), device_id_type=MESH)
    pl.semaphore_wait(barrier, 10)

    def own_copy(src, dst, send, recv, step):
        if step == 0:
            return remote(src, dst.at[z, c], send.at[0], recv.at[z, c], dp, z * 2 + oc)
        return remote(src, dst.at[z, c], send.at[step], recv.at[z, c], dp, block_at(step) * 2 + c)

    def hand_on(dst, send, recv, blk):
        return remote(dst.at[blk, c], dst.at[blk, c], send.at[blk], recv.at[blk, c], dp, z * 2 + oc)

    def arrived(dst, recv, send, blk, core):
        remote(dst.at[blk, core], dst.at[blk, core], send.at[0], recv.at[blk, core], dp, z * 2 + oc).wait_recv()

    def wt_copy(k):
        return remote(wt_ref, wt_all.at[ex], wt_s.at[k], wt_r.at[ex], dp, (ex + k) % 8)

    for step in range(4):
        own_copy(tok_ref, tok_all, tok_s, tok_r, step).start()
    for k in range(1, 8):
        wt_copy(k).start()
    tok_all[z, c] = tok_ref[...]
    grd_all[z, c] = grad_ref[...]
    wt_all[ex] = wt_ref[...]
    own_copy(grad_ref, grd_all, grd_s, grd_r, 0).start()

    def share_out(part, into, send, recv, blk, k):
        to = peer_at(k)
        return remote(part.at[blk, to], into.at[blk, dp], send.at[blk, k], recv.at[blk, dp], to, ex)

    def spread(full, send, recv, blk, k):
        return remote(full.at[blk, dp], full.at[blk, dp], send.at[blk, k], recv.at[blk, dp], peer_at(k), ex)

    def landed(into, send, recv, blk):
        for k in range(1, PEERS):
            src = peer_at(k)
            remote(into.at[blk, src], into.at[blk, src], send.at[blk, k], recv.at[blk, src], src, ex).wait_recv()

    def gate_up(step):
        blk = block_at(step)
        if step > 0:
            arrived(tok_all, tok_r, tok_s, blk, c)
            hand_on(tok_all, tokf_s, tok_r, blk).start()
            own_copy(grad_ref, grd_all, grd_s, grd_r, step).start()
        arrived(tok_all, tok_r, tok_s, blk, oc)

        @pl.loop(0, units // TILE)
        def _(j):
            cols = pl.ds(pl.multiple_of(j * TILE, TILE), TILE)
            more = pl.ds(pl.multiple_of(units + j * TILE, TILE), TILE)
            x = tok_all[blk].reshape(both, width)
            gu_part[blk, :, :, cols] = jnp.dot(x, wg_ref[:, cols], preferred_element_type=f32).astype(bf16).reshape(PEERS, share, TILE)
            gu_part[blk, :, :, more] = jnp.dot(x, wu_ref[:, cols], preferred_element_type=f32).astype(bf16).reshape(PEERS, share, TILE)

        for k in range(1, PEERS):
            share_out(gu_part, gu_in, gu_s, gu_r, blk, k).start()

    for step in range(4):
        gate_up(step)

    for k in range(1, 8):
        src = (ex + k) % 8
        remote(wt_ref, wt_all.at[src], wt_s.at[k], wt_r.at[src], dp, src).wait_recv()
    diagonal = lax.broadcasted_iota(jnp.int32, (128, 128), 0) == lax.broadcasted_iota(jnp.int32, (128, 128), 1)
    for blk in range(4):
        for core in range(2):
            line = wt_all[blk * 2 + core, pl.ds(ex, 1), :]
            column = jnp.sum(jnp.where(diagonal, line, 0.0), axis=1, keepdims=True)
            wcol[blk, core] = jnp.broadcast_to(column[:rows], (rows, 128))

    def hidden_grads(step):
        blk = block_at(step)
        if step > 0:
            arrived(grd_all, grd_r, grd_s, blk, c)
            hand_on(grd_all, grdf_s, grd_r, blk).start()
        arrived(grd_all, grd_r, grd_s, blk, oc)
        w = wcol[blk].reshape(both, 128)[:, :1]
        pg_all[blk] = (w * grd_all[blk].reshape(both, width).astype(f32)).astype(bf16)

        @pl.loop(0, units // TILE)
        def _(j):
            cols = pl.ds(pl.multiple_of(j * TILE, TILE), TILE)
            part = contract_last(pg_all[blk], wd_ref[cols, :])
            hg_part[blk, :, :, cols] = part.astype(bf16).reshape(PEERS, share, TILE)

        for k in range(1, PEERS):
            share_out(hg_part, hg_in, hg_s, hg_r, blk, k).start()

    def make_hidden(step):
        blk = block_at(step)
        landed(gu_in, gu_s, gu_r, blk)
        gu_in[blk, dp] = gu_part[blk, dp]
        both_pre = jnp.sum(gu_in[blk].astype(f32), axis=0)
        gate = both_pre[:, :units]
        up = both_pre[:, units:]
        gpre[blk] = gate
        upre[blk] = up
        hid_all[blk, dp] = (gate * jax.nn.sigmoid(gate) * up).astype(bf16)
        for k in range(1, PEERS):
            spread(hid_all, hid_s, hid_r, blk, k).start()

    def make_grads(step):
        blk = block_at(step)
        landed(hg_in, hg_s, hg_r, blk)
        hg_in[blk, dp] = hg_part[blk, dp]
        hgrad = jnp.sum(hg_in[blk].astype(f32), axis=0)
        gate = gpre[blk]
        s = jax.nn.sigmoid(gate)
        dgu_all[blk, dp, :, :units] = (hgrad * upre[blk] * s * (1.0 + gate * (1.0 - s))).astype(bf16)
        dgu_all[blk, dp, :, units:] = (hgrad * (gate * s)).astype(bf16)
        for k in range(1, PEERS):
            spread(dgu_all, dgu_s, dgu_r, blk, k).start()

    def to_partner(full, into, send, recv, blk):
        return remote(full.at[blk, oc], into.at[blk], send.at[blk], recv.at[blk], dp, z * 2 + oc)

    def home(total, into, send, recv, blk):
        return remote(total.at[blk], into.at[z], send.at[blk], recv.at[z], dp, blk * 2 + c)

    def expert_rows(step):
        blk = block_at(step)
        landed(hid_all, hid_s, hid_r, blk)
        w = wcol[blk].reshape(both, 128)[:, :1]

        @pl.loop(0, width // TILE)
        def _(j):
            cols = pl.ds(pl.multiple_of(j * TILE, TILE), TILE)
            h = hid_all[blk].reshape(both, units)
            part = jnp.dot(h, wd_ref[:, cols], preferred_element_type=f32).astype(bf16)
            eo[blk, :, :, cols] = (w * part.astype(f32)).astype(bf16).reshape(2, rows, TILE)

        to_partner(eo, eo_in, eo_s, eo_r, blk).start()

    def token_rows(step):
        blk = block_at(step)
        landed(dgu_all, dgu_s, dgu_r, blk)

        @pl.loop(0, width // TILE)
        def _(j):
            cols = pl.ds(pl.multiple_of(j * TILE, TILE), TILE)
            part = contract_last(dgu_all[blk, :, :, :units].reshape(both, units), wg_ref[cols, :])
            part += contract_last(dgu_all[blk, :, :, units:].reshape(both, units), wu_ref[cols, :])
            tg[blk, :, :, cols] = part.astype(bf16).reshape(2, rows, TILE)

        to_partner(tg, tg_in, tg_s, tg_r, blk).start()

    def pair_sum(full, into, total, send, recv, zin, zsend, zrecv, step):
        blk = block_at(step)
        to_partner(full, into, send, recv, blk).wait_recv()
        total[blk] = (full[blk, c].astype(f32) + into[blk].astype(f32)).astype(bf16)
        if step > 0:
            home(total, zin, zsend, zrecv, blk).start()

    def finish(total, zin, zsend, zrecv, result):
        for step in range(1, 4):
            blk = block_at(step)
            remote(total.at[blk], zin.at[blk], zsend.at[blk], zrecv.at[blk], dp, blk * 2 + c).wait_recv()
        zin[z] = total[z]
        result[...] = jnp.sum(zin[...].astype(f32), axis=0).astype(bf16)

    order = (1, 2, 3, 0)
    for step in range(4):
        hidden_grads(step)
        make_hidden(step)
    for step in range(4):
        make_grads(step)
        expert_rows(step)
    for step in order:
        pair_sum(eo, eo_in, eo_sum, eo_s, eo_r, eo_z, eoz_s, eoz_r, step)

    @pl.loop(0, units // TILE)
    def _(j):
        cols = pl.ds(pl.multiple_of(j * TILE, TILE), TILE)
        h = hid_all[:, :, :, cols].reshape(BLOCKS * both, TILE)
        dg_ref[cols, :] = contract_rows(h, pg_all[...].reshape(BLOCKS * both, width)).astype(bf16)

    for step in range(4):
        token_rows(step)
        if step > 0:
            pair_sum(tg, tg_in, tg_sum, tg_s, tg_r, tg_z, tgz_s, tgz_r, step - 1)
    pair_sum(tg, tg_in, tg_sum, tg_s, tg_r, tg_z, tgz_s, tgz_r, 3)

    @pl.loop(0, width // TILE)
    def _(j):
        cols = pl.ds(pl.multiple_of(j * TILE, TILE), TILE)
        x = tok_all[:, :, :, cols].reshape(BLOCKS * both, TILE)
        gg_ref[cols, :] = contract_rows(x, dgu_all[:, :, :, :units].reshape(BLOCKS * both, units)).astype(bf16)
        ug_ref[cols, :] = contract_rows(x, dgu_all[:, :, :, units:].reshape(BLOCKS * both, units)).astype(bf16)

    finish(eo_sum, eo_z, eoz_s, eoz_r, out_ref)
    finish(tg_sum, tg_z, tgz_s, tgz_r, tgrad_ref)

    for step in range(4):
        blk = block_at(step)
        own_copy(tok_ref, tok_all, tok_s, tok_r, step).wait_send()
        own_copy(grad_ref, grd_all, grd_s, grd_r, step).wait_send()
        if step > 0:
            hand_on(tok_all, tokf_s, tok_r, blk).wait_send()
            hand_on(grd_all, grdf_s, grd_r, blk).wait_send()
            home(eo_sum, eo_z, eoz_s, eoz_r, blk).wait_send()
            home(tg_sum, tg_z, tgz_s, tgz_r, blk).wait_send()
        to_partner(eo, eo_in, eo_s, eo_r, blk).wait_send()
        to_partner(tg, tg_in, tg_s, tg_r, blk).wait_send()
        for k in range(1, PEERS):
            share_out(gu_part, gu_in, gu_s, gu_r, blk, k).wait_send()
            share_out(hg_part, hg_in, hg_s, hg_r, blk, k).wait_send()
            spread(hid_all, hid_s, hid_r, blk, k).wait_send()
            spread(dgu_all, dgu_s, dgu_r, blk, k).wait_send()
    for k in range(1, 8):
        wt_copy(k).wait_send()


def kernel_body(tokens, expert_ids, gate_probs, gate_weight, up_weight, down_weight, out_grad):
    rows, width = tokens.shape
    units = gate_weight.shape[2]
    share = 2 * rows // PEERS
    weights = gate_probs / jnp.sum(gate_probs, axis=1, keepdims=True)
    named = expert_ids[:, :, None] == jnp.arange(8, dtype=jnp.int32)[None, None, :]
    by_expert = jnp.sum(jnp.where(named, weights[:, :, None], 0.0), axis=1)
    lines = jnp.pad(by_expert.T, ((0, 0), (0, 128 - rows)))
    bf16 = jnp.bfloat16
    f32 = jnp.float32

    def vm(*shape, dtype=bf16):
        return pltpu.VMEM(shape, dtype)

    def sem(*shape):
        return pltpu.SemaphoreType.DMA(shape)

    whole = pl.BlockSpec(memory_space=pltpu.VMEM)
    shapes = [(rows, width), (rows, width), (width, units), (width, units), (units, width)]
    flops = 2 * 9 * 8 * rows * width * units
    results = pl.pallas_call(
        layer_kernel,
        out_shape=[jax.ShapeDtypeStruct(shape, bf16) for shape in shapes],
        in_specs=[whole] * 6,
        out_specs=[whole] * 5,
        scratch_shapes=[
            vm(4, 2, rows, width), vm(4, 2, rows, width), vm(8, 8, 128, dtype=f32),
            vm(4, 2, rows, 128, dtype=f32), vm(4, 2 * rows, width),
            vm(4, PEERS, share, 2 * units), vm(4, PEERS, share, 2 * units),
            vm(4, PEERS, share, units), vm(4, PEERS, share, units),
            vm(4, share, units, dtype=f32), vm(4, share, units, dtype=f32),
            vm(4, PEERS, share, units), vm(4, PEERS, share, 2 * units),
            vm(4, 2, rows, width), vm(4, rows, width), vm(4, rows, width), vm(4, rows, width),
            vm(4, 2, rows, width), vm(4, rows, width), vm(4, rows, width), vm(4, rows, width),
            sem(4), sem(4, 2), sem(4), sem(4, 2), sem(4), sem(4), sem(8), sem(8),
            sem(4, 4), sem(4, 4), sem(4, 4), sem(4, 4), sem(4, 4), sem(4, 4), sem(4, 4), sem(4, 4),
            sem(4), sem(4), sem(4), sem(4), sem(4), sem(4), sem(4), sem(4),
        ],
        compiler_params=pltpu.CompilerParams(
            collective_id=0, has_side_effects=True, vmem_limit_bytes=56 * 1024 * 1024
        ),
        cost_estimate=pl.CostEstimate(flops=flops, bytes_accessed=12_000_000, transcendentals=0),
        name="moe_layer",
    )(tokens, out_grad, lines, gate_weight[0], up_weight[0], down_weight[0])
    layer_out, token_grad, gate_grad, up_grad, down_grad = results
    return layer_out, token_grad, gate_grad[None], up_grad[None], down_grad[None]


def body(tokens, expert_ids, *rest):
    groups = lax.axis_size("expert")
    if expert_ids.shape[1] == groups:
        fits = tokens.shape[0] % 32 == 0 and tokens.shape[0] <= 128
        if groups == 8 and lax.axis_size("dp") == 4 and fits:
            return kernel_body(tokens, expert_ids, *rest)
        return dense_body(tokens, expert_ids, *rest)
    return sparse_body(tokens, expert_ids, *rest)


def solution(mesh):
    placed = (
        P("expert", "dp"),
        P("expert", None),
        P("expert", None),
        P("expert", "dp", None),
        P("expert", "dp", None),
        P("expert", None, "dp"),
        P("expert", "dp"),
    )
    return jax.shard_map(
        body,
        mesh=mesh,
        in_specs=placed,
        out_specs=(
            P("expert", "dp"),
            P("expert", "dp"),
            P("expert", "dp", None),
            P("expert", "dp", None),
            P("expert", None, "dp"),
        ),
        check_vma=False,
    )
```

```python
import jax
import jax.numpy as jnp
from jax import lax
from jax.experimental import pallas as pl
from jax.experimental.pallas import tpu as pltpu
from jax.sharding import PartitionSpec as P


def rounded(values):
    return lax.optimization_barrier(values.astype(jnp.bfloat16)).astype(jnp.float32)


def contract_last(first_op, second_op):
    return lax.dot_general(
        first_op, second_op, (((1,), (1,)), ((), ())), preferred_element_type=jnp.float32
    )


def contract_rows(first_op, second_op):
    return lax.dot_general(
        first_op, second_op, (((0,), (0,)), ((), ())), preferred_element_type=jnp.float32
    )


def swish_grads(grad_in, gate_pre, up_pre):
    sigmoid_gate = jax.nn.sigmoid(gate_pre)
    gate_pre_grad = (
        grad_in * up_pre * sigmoid_gate * (1.0 + gate_pre * (1.0 - sigmoid_gate))
    ).astype(jnp.bfloat16)
    up_pre_grad = (grad_in * jax.nn.silu(gate_pre)).astype(jnp.bfloat16)
    return (gate_pre_grad, up_pre_grad)


def send_back(values):
    return lax.all_to_all(values, "expert", split_axis=0, concat_axis=0, tiled=True)


def sparse_body(tokens, expert_ids, gate_probs, gate_weight, up_weight, down_weight, out_grad):
    tok_rows, width_part = tokens.shape
    top_count = expert_ids.shape[1]
    groups = lax.axis_size("expert")
    capacity = min(tok_rows, 4 * tok_rows * top_count // (3 * groups))
    slot_count = groups * capacity
    pair_count = tok_rows * top_count
    hidden_units = gate_weight.shape[2]
    w_gate = gate_weight[0]
    w_up = up_weight[0]
    w_down = down_weight[0]
    weights = gate_probs / jnp.sum(gate_probs, axis=1, keepdims=True)
    flat_ids = expert_ids.reshape(pair_count)
    onehot = (flat_ids[:, None] == jnp.arange(groups, dtype=jnp.int32)[None, :]).astype(jnp.int32)
    earlier = jnp.cumsum(onehot, axis=0) - onehot
    position = jnp.sum(earlier * onehot, axis=1)
    slot_of_pair = flat_ids * capacity + position
    pair_of_slot = (
        jnp.full((slot_count,), pair_count, jnp.int32)
        .at[slot_of_pair]
        .set(jnp.arange(pair_count, dtype=jnp.int32))
    )
    token_of_slot = pair_of_slot // top_count
    zero_row = jnp.zeros((1, width_part), jnp.bfloat16)
    send_rows = jnp.concatenate([tokens, zero_row], axis=0)[token_of_slot].reshape(
        groups, capacity, width_part
    )

    def run_blocks(step_fn, initial):
        return step_fn(0, slot_count, initial)

    expert_rows = lax.all_to_all(
        send_rows, "expert", split_axis=0, concat_axis=0, tiled=True
    ).reshape(slot_count, width_part)

    def gate_up_step(offset, length, current):
        gate_acc = rounded(jnp.dot(expert_rows, w_gate, preferred_element_type=jnp.float32))
        up_acc = rounded(jnp.dot(expert_rows, w_up, preferred_element_type=jnp.float32))
        return (gate_acc, up_acc)

    zero_hidden = jnp.zeros((slot_count, hidden_units), jnp.float32)
    gate_part, up_part = run_blocks(gate_up_step, (zero_hidden, zero_hidden))
    gate_pre, up_pre = (
        lax.psum(gate_part.astype(jnp.bfloat16), "dp").astype(jnp.float32),
        lax.psum(up_part.astype(jnp.bfloat16), "dp").astype(jnp.float32),
    )
    hidden = (jax.nn.silu(gate_pre) * up_pre).astype(jnp.bfloat16)

    def down_step(offset, length, current):
        result_rows = jnp.dot(hidden, w_down, preferred_element_type=jnp.float32).astype(
            jnp.bfloat16
        )
        return result_rows

    expert_out = run_blocks(down_step, jnp.zeros((slot_count, width_part), jnp.bfloat16))
    returned = send_back(expert_out.reshape(groups, capacity, width_part)).reshape(
        slot_count, width_part
    )
    pair_out = returned[slot_of_pair].reshape(tok_rows, top_count, width_part)
    layer_out = jnp.sum(weights[:, :, None] * pair_out.astype(jnp.float32), axis=1).astype(
        jnp.bfloat16
    )
    pair_grad = (
        (weights[:, :, None] * out_grad[:, None, :].astype(jnp.float32))
        .astype(jnp.bfloat16)
        .reshape(pair_count, width_part)
    )
    send_grads = jnp.concatenate([pair_grad, zero_row], axis=0)[pair_of_slot].reshape(
        groups, capacity, width_part
    )
    grad_rows = lax.all_to_all(
        send_grads, "expert", split_axis=0, concat_axis=0, tiled=True
    ).reshape(slot_count, width_part)

    def hidden_grad_step(offset, length, current):
        hidden_acc = rounded(contract_last(grad_rows, w_down))
        down_acc = contract_rows(hidden, grad_rows)
        return (hidden_acc, down_acc)

    hidden_grad_part, down_total = run_blocks(
        hidden_grad_step, (zero_hidden, jnp.zeros((hidden_units, width_part), jnp.float32))
    )
    hidden_grad = lax.psum(hidden_grad_part.astype(jnp.bfloat16), "dp").astype(jnp.float32)
    gate_pre_grad, up_pre_grad = swish_grads(hidden_grad, gate_pre, up_pre)

    def token_step(offset, length, current):
        pair_token = (
            contract_last(gate_pre_grad, w_gate) + contract_last(up_pre_grad, w_up)
        ).astype(jnp.bfloat16)
        gate_acc = contract_rows(expert_rows, gate_pre_grad)
        up_acc = contract_rows(expert_rows, up_pre_grad)
        return (pair_token, gate_acc, up_acc)

    zero_weight = jnp.zeros((width_part, hidden_units), jnp.float32)
    token_part, gate_total, up_total = run_blocks(
        token_step, (jnp.zeros((slot_count, width_part), jnp.bfloat16), zero_weight, zero_weight)
    )
    returned_grad = send_back(token_part.reshape(groups, capacity, width_part)).reshape(
        slot_count, width_part
    )
    pair_token_grad = returned_grad[slot_of_pair].reshape(tok_rows, top_count, width_part)
    token_grad = jnp.sum(pair_token_grad.astype(jnp.float32), axis=1).astype(jnp.bfloat16)
    return (
        layer_out,
        token_grad,
        gate_total.astype(jnp.bfloat16)[None],
        up_total.astype(jnp.bfloat16)[None],
        down_total.astype(jnp.bfloat16)[None],
    )


def dense_body(tokens, expert_ids, gate_probs, gate_weight, up_weight, down_weight, out_grad):
    groups = lax.axis_size("expert")
    me = lax.axis_index("expert")
    w_gate = gate_weight[0]
    w_up = up_weight[0]
    w_down = down_weight[0]
    weights = gate_probs / jnp.sum(gate_probs, axis=1, keepdims=True)
    named = expert_ids[:, :, None] == jnp.arange(groups, dtype=jnp.int32)[None, None, :]
    by_expert = jnp.sum(jnp.where(named, weights[:, :, None], 0.0), axis=1)
    all_weights = lax.all_gather(by_expert, "expert", axis=0, tiled=True)
    mine = jnp.arange(groups, dtype=jnp.int32)[None, :] == me
    weight = jnp.sum(jnp.where(mine, all_weights, 0.0), axis=1, keepdims=True)
    rows = lax.all_gather(tokens, "expert", axis=0, tiled=True)
    grads = lax.all_gather(out_grad, "expert", axis=0, tiled=True)
    pair_grad = (weight * grads.astype(jnp.float32)).astype(jnp.bfloat16)

    def total(values):
        return lax.psum(values.astype(jnp.bfloat16), "dp").astype(jnp.float32)

    gate_pre = total(jnp.dot(rows, w_gate, preferred_element_type=jnp.float32))
    up_pre = total(jnp.dot(rows, w_up, preferred_element_type=jnp.float32))
    hidden_grad = total(contract_last(pair_grad, w_down))
    hidden = (jax.nn.silu(gate_pre) * up_pre).astype(jnp.bfloat16)
    expert_out = jnp.dot(hidden, w_down, preferred_element_type=jnp.float32)
    layer_out = lax.psum_scatter(
        (weight * expert_out).astype(jnp.bfloat16), "expert", scatter_dimension=0, tiled=True
    )
    gate_pre_grad, up_pre_grad = swish_grads(hidden_grad, gate_pre, up_pre)
    pair_token = contract_last(gate_pre_grad, w_gate) + contract_last(up_pre_grad, w_up)
    token_grad = lax.psum_scatter(
        pair_token.astype(jnp.bfloat16), "expert", scatter_dimension=0, tiled=True
    )
    return (
        layer_out,
        token_grad,
        contract_rows(rows, gate_pre_grad).astype(jnp.bfloat16)[None],
        contract_rows(rows, up_pre_grad).astype(jnp.bfloat16)[None],
        contract_rows(hidden, pair_grad).astype(jnp.bfloat16)[None],
    )


TILE = 256
BLOCKS = 4
PEERS = 4
MESH = pl.DeviceIdType.MESH


def layer_kernel(
    tok_ref, grad_ref, ids_ref, probs_ref, wg_hbm, wu_hbm, wd_hbm,
    out_ref, tgrad_ref, gg_hbm, ug_hbm, dg_hbm,
    wg_ref, wu_ref, wd_ref, gg_ref, ug_ref, dg_ref,
    tok_all, grd_all, wt_ref, wt_all, wcol, pg_all,
    gu_part, gu_1x, gu_1y, gu_sx, gu_sy, gu_2x, gu_2y,
    hg_part, hg_1x, hg_1y, hg_sx, hg_sy, hg_2x, hg_2y,
    gpre, upre, hid_all, dgu_all,
    eo, eo_in, eo_sum, eo_z, tg, tg_in, tg_sum, tg_z,
    w_s, g_s, d_s,
    tok_s, tok_r, grd_s, grd_r, tokf_s, grdf_s, wt_s, wt_r,
    gu_s, gu_r, hg_s, hg_r, hid_s, hid_r, dgu_s, dgu_r,
    eo_s, eo_r, eoz_s, eoz_r, tg_s, tg_r, tgz_s, tgz_r,
):
    dp = lax.axis_index("dp")
    ex = lax.axis_index("expert")
    z = ex // 2
    c = ex % 2
    oc = 1 - c
    y = dp // 2
    x = dp % 2
    oy = 1 - y
    ox = 1 - x
    dp_x = y * 2 + ox
    dp_y = oy * 2 + x
    rows, width = tok_ref.shape
    units = wg_ref.shape[1]
    share = gu_part.shape[3]
    both = 2 * rows
    bf16 = jnp.bfloat16
    f32 = jnp.float32
    loads = [
        pltpu.make_async_copy(src.at[0], dst, w_s.at[n])
        for n, (src, dst) in enumerate(((wg_hbm, wg_ref), (wu_hbm, wu_ref), (wd_hbm, wd_ref)))
    ]
    for load in loads:
        load.start()

    def block_at(step):
        return ((z // 2 + step // 2) % 2) * 2 + (z + step) % 2

    def remote(src, dst, send, recv, to_dp, to_ex):
        return pltpu.make_async_remote_copy(
            src_ref=src, dst_ref=dst, send_sem=send, recv_sem=recv,
            device_id=(to_dp, to_ex), device_id_type=MESH,
        )

    barrier = pltpu.get_barrier_semaphore()
    for k in range(1, 8):
        pl.semaphore_signal(barrier, inc=1, device_id=(dp, (ex + k) % 8), device_id_type=MESH)
    pl.semaphore_signal(barrier, inc=1, device_id=(dp_x, ex), device_id_type=MESH)
    pl.semaphore_signal(barrier, inc=1, device_id=(dp_y, ex), device_id_type=MESH)

    probs = probs_ref[...]
    weights = probs / jnp.sum(probs, axis=1, keepdims=True)
    lane = lax.broadcasted_iota(jnp.int32, (rows, 128), 1)
    table = jnp.zeros((rows, 128), f32)
    for e in range(8):
        named = jnp.sum(jnp.where(ids_ref[...] == e, weights, 0.0), axis=1, keepdims=True)
        table = jnp.where(lane == e, named, table)
    table = jnp.concatenate([table, jnp.zeros((128 - rows, 128), f32)], axis=0) if rows < 128 else table
    wt_ref[...] = table.T[:8]
    pl.semaphore_wait(barrier, 9)

    def own_copy(src, dst, send, recv, step):
        if step == 0:
            return remote(src, dst.at[z, c], send.at[0], recv.at[z, c], dp, z * 2 + oc)
        return remote(src, dst.at[z, c], send.at[step], recv.at[z, c], dp, block_at(step) * 2 + c)

    def hand_on(dst, send, recv, blk):
        return remote(dst.at[blk, c], dst.at[blk, c], send.at[blk], recv.at[blk, c], dp, z * 2 + oc)

    def arrived(dst, recv, send, blk, core):
        remote(dst.at[blk, core], dst.at[blk, core], send.at[0], recv.at[blk, core], dp, z * 2 + oc).wait_recv()

    def wt_copy(k):
        return remote(wt_ref, wt_all.at[ex], wt_s.at[k], wt_r.at[ex], dp, (ex + k) % 8)

    for step in range(4):
        own_copy(tok_ref, tok_all, tok_s, tok_r, step).start()
    for k in range(1, 8):
        wt_copy(k).start()
    tok_all[z, c] = tok_ref[...]
    grd_all[z, c] = grad_ref[...]
    wt_all[ex] = wt_ref[...]
    own_copy(grad_ref, grd_all, grd_s, grd_r, 0).start()

    def first_x(part, into, send, recv, blk):
        half = into.shape[-1]
        return remote(part.at[blk, :, ox, :, pl.ds(0, half)], into.at[blk], send.at[0, blk], recv.at[0, blk], dp_x, ex)

    def first_y(part, into, send, recv, blk):
        half = into.shape[-1]
        return remote(part.at[blk, oy, :, :, pl.ds(half, half)], into.at[blk], send.at[1, blk], recv.at[1, blk], dp_y, ex)

    def second_x(total, into, send, recv, blk):
        return remote(total.at[blk], into.at[blk], send.at[2, blk], recv.at[2, blk], dp_x, ex)

    def second_y(total, into, send, recv, blk):
        return remote(total.at[blk], into.at[blk], send.at[3, blk], recv.at[3, blk], dp_y, ex)

    def pass_on(part, in_x, in_y, sum_x, sum_y, to_x, to_y, send, recv, step):
        blk = block_at(step)
        half = in_x.shape[-1]
        first_x(part, in_x, send, recv, blk).wait_recv()
        sum_y[blk] = (part[blk, oy, x, :, :half].astype(f32) + in_x[blk, oy].astype(f32)).astype(bf16)
        second_y(sum_y, to_y, send, recv, blk).start()
        first_y(part, in_y, send, recv, blk).wait_recv()
        sum_x[blk] = (part[blk, y, ox, :, half:].astype(f32) + in_y[blk, ox].astype(f32)).astype(bf16)
        second_x(sum_x, to_x, send, recv, blk).start()

    def summed(part, in_x, in_y, sum_x, sum_y, to_x, to_y, send, recv, blk):
        half = in_x.shape[-1]
        second_y(sum_y, to_y, send, recv, blk).wait_recv()
        second_x(sum_x, to_x, send, recv, blk).wait_recv()
        low = part[blk, y, x, :, :half].astype(f32) + in_x[blk, y].astype(f32) + to_y[blk].astype(f32)
        high = part[blk, y, x, :, half:].astype(f32) + in_y[blk, x].astype(f32) + to_x[blk].astype(f32)
        return low, high

    def spread(full, send, recv, blk, kind):
        half = full.shape[-1] // 2
        low = pl.ds(0, half)
        high = pl.ds(half, half)
        if kind == 0:
            src, to = full.at[blk, y, x], dp_x
        elif kind == 1:
            src, to = full.at[blk, y, x], dp_y
        elif kind == 2:
            src, to = full.at[blk, oy, x, :, low], dp_x
        else:
            src, to = full.at[blk, y, ox, :, high], dp_y
        return remote(src, src, send.at[kind, blk], recv.at[kind, blk], to, ex)

    def spread_got(full, send, recv, blk, kind):
        half = full.shape[-1] // 2
        if kind == 0:
            dst = full.at[blk, y, ox]
        elif kind == 1:
            dst = full.at[blk, oy, x]
        else:
            dst = full.at[blk, oy, ox, :, pl.ds(0 if kind == 2 else half, half)]
        remote(dst, dst, send.at[kind, blk], recv.at[kind, blk], dp_x, ex).wait_recv()

    def hand_over(full, send, recv, step):
        blk = block_at(step)
        spread_got(full, send, recv, blk, 1)
        spread(full, send, recv, blk, 2).start()
        spread_got(full, send, recv, blk, 0)
        spread(full, send, recv, blk, 3).start()

    def landed(full, send, recv, blk):
        spread_got(full, send, recv, blk, 2)
        spread_got(full, send, recv, blk, 3)

    gu = (gu_part, gu_1x, gu_1y, gu_sx, gu_sy, gu_2x, gu_2y, gu_s, gu_r)
    hg = (hg_part, hg_1x, hg_1y, hg_sx, hg_sy, hg_2x, hg_2y, hg_s, hg_r)

    def gate_up(step):
        blk = block_at(step)
        if step > 0:
            arrived(tok_all, tok_r, tok_s, blk, c)
            hand_on(tok_all, tokf_s, tok_r, blk).start()
            own_copy(grad_ref, grd_all, grd_s, grd_r, step).start()
        arrived(tok_all, tok_r, tok_s, blk, oc)

        @pl.loop(0, units // TILE)
        def _(j):
            cols = pl.ds(pl.multiple_of(j * TILE, TILE), TILE)
            more = pl.ds(pl.multiple_of(units + j * TILE, TILE), TILE)
            t = tok_all[blk].reshape(both, width)
            gu_part[blk, :, :, :, cols] = jnp.dot(t, wg_ref[:, cols], preferred_element_type=f32).astype(bf16).reshape(2, 2, share, TILE)
            gu_part[blk, :, :, :, more] = jnp.dot(t, wu_ref[:, cols], preferred_element_type=f32).astype(bf16).reshape(2, 2, share, TILE)

        first_x(gu_part, gu_1x, gu_s, gu_r, blk).start()
        first_y(gu_part, gu_1y, gu_s, gu_r, blk).start()

    loads[0].wait()
    loads[1].wait()
    gate_up(0)
    gate_up(1)
    pass_on(*gu, 0)
    gate_up(2)
    pass_on(*gu, 1)
    gate_up(3)
    pass_on(*gu, 2)
    loads[2].wait()

    for k in range(1, 8):
        src = (ex + k) % 8
        remote(wt_ref, wt_all.at[src], wt_s.at[k], wt_r.at[src], dp, src).wait_recv()
    diagonal = lax.broadcasted_iota(jnp.int32, (128, 128), 0) == lax.broadcasted_iota(jnp.int32, (128, 128), 1)
    for blk in range(4):
        for core in range(2):
            line = wt_all[blk * 2 + core, pl.ds(ex, 1), :]
            column = jnp.sum(jnp.where(diagonal, line, 0.0), axis=1, keepdims=True)
            wcol[blk, core] = jnp.broadcast_to(column[:rows], (rows, 128))

    def hidden_grads(step):
        blk = block_at(step)
        if step > 0:
            arrived(grd_all, grd_r, grd_s, blk, c)
            hand_on(grd_all, grdf_s, grd_r, blk).start()
        arrived(grd_all, grd_r, grd_s, blk, oc)
        w = wcol[blk].reshape(both, 128)[:, :1]
        pg_all[blk] = (w * grd_all[blk].reshape(both, width).astype(f32)).astype(bf16)

        @pl.loop(0, units // TILE)
        def _(j):
            cols = pl.ds(pl.multiple_of(j * TILE, TILE), TILE)
            part = contract_last(pg_all[blk], wd_ref[cols, :])
            hg_part[blk, :, :, :, cols] = part.astype(bf16).reshape(2, 2, share, TILE)

        first_x(hg_part, hg_1x, hg_s, hg_r, blk).start()
        first_y(hg_part, hg_1y, hg_s, hg_r, blk).start()

    def make_hidden(step):
        blk = block_at(step)
        gate, up = summed(*gu, blk)
        gpre[blk] = gate
        upre[blk] = up
        hid_all[blk, y, x] = (gate * jax.nn.sigmoid(gate) * up).astype(bf16)
        for kind in range(2):
            spread(hid_all, hid_s, hid_r, blk, kind).start()

    def make_grads(step):
        blk = block_at(step)
        hgrad = jnp.concatenate(summed(*hg, blk), axis=1)
        gate = gpre[blk]
        s = jax.nn.sigmoid(gate)
        dgu_all[blk, y, x, :, :units] = (hgrad * upre[blk] * s * (1.0 + gate * (1.0 - s))).astype(bf16)
        dgu_all[blk, y, x, :, units:] = (hgrad * (gate * s)).astype(bf16)
        for kind in range(2):
            spread(dgu_all, dgu_s, dgu_r, blk, kind).start()

    def to_partner(full, into, send, recv, blk):
        return remote(full.at[blk, oc], into.at[blk], send.at[blk], recv.at[blk], dp, z * 2 + oc)

    def home(total, into, send, recv, blk):
        return remote(total.at[blk], into.at[z], send.at[blk], recv.at[z], dp, blk * 2 + c)

    def expert_rows(step):
        blk = block_at(step)
        landed(hid_all, hid_s, hid_r, blk)
        w = wcol[blk].reshape(both, 128)[:, :1]

        @pl.loop(0, width // TILE)
        def _(j):
            cols = pl.ds(pl.multiple_of(j * TILE, TILE), TILE)
            h = hid_all[blk].reshape(both, units)
            part = jnp.dot(h, wd_ref[:, cols], preferred_element_type=f32).astype(bf16)
            eo[blk, :, :, cols] = (w * part.astype(f32)).astype(bf16).reshape(2, rows, TILE)

        to_partner(eo, eo_in, eo_s, eo_r, blk).start()

    def token_rows(step):
        blk = block_at(step)
        landed(dgu_all, dgu_s, dgu_r, blk)

        @pl.loop(0, width // TILE)
        def _(j):
            cols = pl.ds(pl.multiple_of(j * TILE, TILE), TILE)
            part = contract_last(dgu_all[blk, :, :, :, :units].reshape(both, units), wg_ref[cols, :])
            part += contract_last(dgu_all[blk, :, :, :, units:].reshape(both, units), wu_ref[cols, :])
            tg[blk, :, :, cols] = part.astype(bf16).reshape(2, rows, TILE)

        to_partner(tg, tg_in, tg_s, tg_r, blk).start()

    def pair_sum(full, into, total, send, recv, zin, zsend, zrecv, step):
        blk = block_at(step)
        to_partner(full, into, send, recv, blk).wait_recv()
        total[blk] = (full[blk, c].astype(f32) + into[blk].astype(f32)).astype(bf16)
        if step > 0:
            home(total, zin, zsend, zrecv, blk).start()

    def finish(total, zin, zsend, zrecv, result):
        for step in range(1, 4):
            blk = block_at(step)
            remote(total.at[blk], zin.at[blk], zsend.at[blk], zrecv.at[blk], dp, blk * 2 + c).wait_recv()
        zin[z] = total[z]
        result[...] = jnp.sum(zin[...].astype(f32), axis=0).astype(bf16)

    def eo_pair(step):
        pair_sum(eo, eo_in, eo_sum, eo_s, eo_r, eo_z, eoz_s, eoz_r, step)

    def tg_pair(step):
        pair_sum(tg, tg_in, tg_sum, tg_s, tg_r, tg_z, tgz_s, tgz_r, step)

    def hid_over(step):
        hand_over(hid_all, hid_s, hid_r, step)

    def dgu_over(step):
        hand_over(dgu_all, dgu_s, dgu_r, step)

    hidden_grads(0)
    pass_on(*gu, 3)
    make_hidden(0)
    make_hidden(1)
    hidden_grads(1)
    pass_on(*hg, 0)
    make_hidden(2)
    hid_over(0)
    make_hidden(3)
    hid_over(1)
    hidden_grads(2)
    pass_on(*hg, 1)
    hid_over(2)
    hidden_grads(3)
    pass_on(*hg, 2)
    hid_over(3)
    pass_on(*hg, 3)
    make_grads(1)
    expert_rows(1)
    make_grads(2)
    expert_rows(2)
    dgu_over(1)
    make_grads(3)
    eo_pair(1)
    expert_rows(3)
    dgu_over(2)
    make_grads(0)
    eo_pair(2)
    token_rows(1)
    eo_pair(3)
    dgu_over(3)
    expert_rows(0)
    tg_pair(1)
    token_rows(2)
    dgu_over(0)

    @pl.loop(0, units // TILE)
    def _(j):
        cols = pl.ds(pl.multiple_of(j * TILE, TILE), TILE)
        h = hid_all[:, :, :, :, cols].reshape(BLOCKS * both, TILE)
        dg_ref[cols, :] = contract_rows(h, pg_all[...].reshape(BLOCKS * both, width)).astype(bf16)

    down_store = pltpu.make_async_copy(dg_ref, dg_hbm, d_s)
    down_store.start()
    eo_pair(0)
    tg_pair(2)
    token_rows(3)
    tg_pair(3)
    token_rows(0)

    def stores(j):
        cols = pl.ds(pl.multiple_of(j * TILE, TILE), TILE)
        return (
            pltpu.make_async_copy(gg_ref.at[cols, :], gg_hbm.at[cols, :], g_s.at[0, j]),
            pltpu.make_async_copy(ug_ref.at[cols, :], ug_hbm.at[cols, :], g_s.at[1, j]),
        )

    @pl.loop(0, width // TILE)
    def _(j):
        cols = pl.ds(pl.multiple_of(j * TILE, TILE), TILE)
        t = tok_all[:, :, :, cols].reshape(BLOCKS * both, TILE)
        gg_ref[cols, :] = contract_rows(t, dgu_all[:, :, :, :, :units].reshape(BLOCKS * both, units)).astype(bf16)
        ug_ref[cols, :] = contract_rows(t, dgu_all[:, :, :, :, units:].reshape(BLOCKS * both, units)).astype(bf16)
        for store in stores(j):
            store.start()

    tg_pair(0)
    finish(eo_sum, eo_z, eoz_s, eoz_r, out_ref)
    finish(tg_sum, tg_z, tgz_s, tgz_r, tgrad_ref)

    for step in range(4):
        blk = block_at(step)
        own_copy(tok_ref, tok_all, tok_s, tok_r, step).wait_send()
        own_copy(grad_ref, grd_all, grd_s, grd_r, step).wait_send()
        if step > 0:
            hand_on(tok_all, tokf_s, tok_r, blk).wait_send()
            hand_on(grd_all, grdf_s, grd_r, blk).wait_send()
            home(eo_sum, eo_z, eoz_s, eoz_r, blk).wait_send()
            home(tg_sum, tg_z, tgz_s, tgz_r, blk).wait_send()
        to_partner(eo, eo_in, eo_s, eo_r, blk).wait_send()
        to_partner(tg, tg_in, tg_s, tg_r, blk).wait_send()
        for part, in_x, in_y, sum_x, sum_y, to_x, to_y, send, recv in (gu, hg):
            first_x(part, in_x, send, recv, blk).wait_send()
            first_y(part, in_y, send, recv, blk).wait_send()
            second_x(sum_x, to_x, send, recv, blk).wait_send()
            second_y(sum_y, to_y, send, recv, blk).wait_send()
        for kind in range(4):
            spread(hid_all, hid_s, hid_r, blk, kind).wait_send()
            spread(dgu_all, dgu_s, dgu_r, blk, kind).wait_send()
    for k in range(1, 8):
        wt_copy(k).wait_send()
    down_store.wait()

    @pl.loop(0, width // TILE)
    def _(j):
        for store in stores(j):
            store.wait()


def store_kernel(*refs):
    sems = refs[-1]
    count = (len(refs) - 1) // 2
    copies = []
    for n in range(count):
        dst = refs[count + n]
        dst = dst.at[0] if len(dst.shape) == 3 else dst
        copies.append(pltpu.make_async_copy(refs[n], dst, sems.at[n]))
    for copy in copies:
        copy.start()
    for copy in copies:
        copy.wait()


def kernel_body(tokens, expert_ids, gate_probs, gate_weight, up_weight, down_weight, out_grad):
    rows, width = tokens.shape
    units = gate_weight.shape[2]
    share = 2 * rows // PEERS
    bf16 = jnp.bfloat16
    f32 = jnp.float32

    def vm(*shape, dtype=bf16):
        return pltpu.VMEM(shape, dtype)

    def sem(*shape):
        return pltpu.SemaphoreType.DMA(shape)

    whole = pl.BlockSpec(memory_space=pltpu.VMEM)
    shapes = [(rows, width), (rows, width), (width, units), (width, units), (units, width)]
    flops = 2 * 9 * 8 * rows * width * units
    anywhere = pl.BlockSpec(memory_space=pl.ANY)

    def exchange(columns):
        half = columns // 2
        return [vm(4, 2, 2, share, columns), vm(4, 2, share, half), vm(4, 2, share, half)] + [
            vm(4, share, half)
        ] * 4

    results = pl.pallas_call(
        layer_kernel,
        out_shape=[jax.ShapeDtypeStruct(shape, bf16) for shape in shapes],
        in_specs=[whole] * 4 + [anywhere] * 3,
        out_specs=[whole] * 2 + [anywhere] * 3,
        scratch_shapes=[
            vm(width, units), vm(width, units), vm(units, width),
            vm(width, units), vm(width, units), vm(units, width),
            vm(4, 2, rows, width), vm(4, 2, rows, width), vm(8, 128, dtype=f32), vm(8, 8, 128, dtype=f32),
            vm(4, 2, rows, 128, dtype=f32), vm(4, 2 * rows, width),
            *exchange(2 * units), *exchange(units),
            vm(4, share, units, dtype=f32), vm(4, share, units, dtype=f32),
            vm(4, 2, 2, share, units), vm(4, 2, 2, share, 2 * units),
            vm(4, 2, rows, width), vm(4, rows, width), vm(4, rows, width), vm(4, rows, width),
            vm(4, 2, rows, width), vm(4, rows, width), vm(4, rows, width), vm(4, rows, width),
            sem(3), sem(2, width // TILE), pltpu.SemaphoreType.DMA,
            sem(4), sem(4, 2), sem(4), sem(4, 2), sem(4), sem(4), sem(8), sem(8),
            sem(4, 4), sem(4, 4), sem(4, 4), sem(4, 4), sem(4, 4), sem(4, 4), sem(4, 4), sem(4, 4),
            sem(4), sem(4), sem(4), sem(4), sem(4), sem(4), sem(4), sem(4),
        ],
        compiler_params=pltpu.CompilerParams(
            collective_id=0, has_side_effects=True, vmem_limit_bytes=48 * 1024 * 1024
        ),
        cost_estimate=pl.CostEstimate(flops=flops, bytes_accessed=12_000_000, transcendentals=0),
        name="moe_layer",
    )(tokens, out_grad, expert_ids, gate_probs, gate_weight, up_weight, down_weight)
    final = shapes[:2] + [(1, *shape) for shape in shapes[2:]]
    return tuple(
        pl.pallas_call(
            store_kernel,
            out_shape=[jax.ShapeDtypeStruct(shape, bf16) for shape in final],
            in_specs=[anywhere] * 5,
            out_specs=[anywhere] * 5,
            scratch_shapes=[sem(5)],
            name="store_results",
        )(*results)
    )


def body(tokens, expert_ids, *rest):
    groups = lax.axis_size("expert")
    if expert_ids.shape[1] == groups:
        fits = tokens.shape[0] % 32 == 0 and tokens.shape[0] <= 128
        if groups == 8 and lax.axis_size("dp") == 4 and fits:
            return kernel_body(tokens, expert_ids, *rest)
        return dense_body(tokens, expert_ids, *rest)
    return sparse_body(tokens, expert_ids, *rest)


def solution(mesh):
    placed = (
        P("expert", "dp"),
        P("expert", None),
        P("expert", None),
        P("expert", "dp", None),
        P("expert", "dp", None),
        P("expert", None, "dp"),
        P("expert", "dp"),
    )
    return jax.shard_map(
        body,
        mesh=mesh,
        in_specs=placed,
        out_specs=(
            P("expert", "dp"),
            P("expert", "dp"),
            P("expert", "dp", None),
            P("expert", "dp", None),
            P("expert", None, "dp"),
        ),
        check_vma=False,
    )
```

```python
import jax
import jax.numpy as jnp
from jax import lax
from jax.experimental import pallas as pl
from jax.experimental.pallas import tpu as pltpu
from jax.sharding import PartitionSpec as P


def rounded(values):
    return lax.optimization_barrier(values.astype(jnp.bfloat16)).astype(jnp.float32)


def contract_last(first_op, second_op):
    return lax.dot_general(
        first_op, second_op, (((1,), (1,)), ((), ())), preferred_element_type=jnp.float32
    )


def contract_rows(first_op, second_op):
    return lax.dot_general(
        first_op, second_op, (((0,), (0,)), ((), ())), preferred_element_type=jnp.float32
    )


def swish_grads(grad_in, gate_pre, up_pre):
    sigmoid_gate = jax.nn.sigmoid(gate_pre)
    gate_pre_grad = (
        grad_in * up_pre * sigmoid_gate * (1.0 + gate_pre * (1.0 - sigmoid_gate))
    ).astype(jnp.bfloat16)
    up_pre_grad = (grad_in * jax.nn.silu(gate_pre)).astype(jnp.bfloat16)
    return (gate_pre_grad, up_pre_grad)


def send_back(values):
    return lax.all_to_all(values, "expert", split_axis=0, concat_axis=0, tiled=True)


def sparse_body(tokens, expert_ids, gate_probs, gate_weight, up_weight, down_weight, out_grad):
    tok_rows, width_part = tokens.shape
    top_count = expert_ids.shape[1]
    groups = lax.axis_size("expert")
    capacity = min(tok_rows, 4 * tok_rows * top_count // (3 * groups))
    slot_count = groups * capacity
    pair_count = tok_rows * top_count
    hidden_units = gate_weight.shape[2]
    w_gate = gate_weight[0]
    w_up = up_weight[0]
    w_down = down_weight[0]
    weights = gate_probs / jnp.sum(gate_probs, axis=1, keepdims=True)
    flat_ids = expert_ids.reshape(pair_count)
    onehot = (flat_ids[:, None] == jnp.arange(groups, dtype=jnp.int32)[None, :]).astype(jnp.int32)
    earlier = jnp.cumsum(onehot, axis=0) - onehot
    position = jnp.sum(earlier * onehot, axis=1)
    slot_of_pair = flat_ids * capacity + position
    pair_of_slot = (
        jnp.full((slot_count,), pair_count, jnp.int32)
        .at[slot_of_pair]
        .set(jnp.arange(pair_count, dtype=jnp.int32))
    )
    token_of_slot = pair_of_slot // top_count
    zero_row = jnp.zeros((1, width_part), jnp.bfloat16)
    send_rows = jnp.concatenate([tokens, zero_row], axis=0)[token_of_slot].reshape(
        groups, capacity, width_part
    )

    def run_blocks(step_fn, initial):
        return step_fn(0, slot_count, initial)

    expert_rows = lax.all_to_all(
        send_rows, "expert", split_axis=0, concat_axis=0, tiled=True
    ).reshape(slot_count, width_part)

    def gate_up_step(offset, length, current):
        gate_acc = rounded(jnp.dot(expert_rows, w_gate, preferred_element_type=jnp.float32))
        up_acc = rounded(jnp.dot(expert_rows, w_up, preferred_element_type=jnp.float32))
        return (gate_acc, up_acc)

    zero_hidden = jnp.zeros((slot_count, hidden_units), jnp.float32)
    gate_part, up_part = run_blocks(gate_up_step, (zero_hidden, zero_hidden))
    gate_pre, up_pre = (
        lax.psum(gate_part.astype(jnp.bfloat16), "dp").astype(jnp.float32),
        lax.psum(up_part.astype(jnp.bfloat16), "dp").astype(jnp.float32),
    )
    hidden = (jax.nn.silu(gate_pre) * up_pre).astype(jnp.bfloat16)

    def down_step(offset, length, current):
        result_rows = jnp.dot(hidden, w_down, preferred_element_type=jnp.float32).astype(
            jnp.bfloat16
        )
        return result_rows

    expert_out = run_blocks(down_step, jnp.zeros((slot_count, width_part), jnp.bfloat16))
    returned = send_back(expert_out.reshape(groups, capacity, width_part)).reshape(
        slot_count, width_part
    )
    pair_out = returned[slot_of_pair].reshape(tok_rows, top_count, width_part)
    layer_out = jnp.sum(weights[:, :, None] * pair_out.astype(jnp.float32), axis=1).astype(
        jnp.bfloat16
    )
    pair_grad = (
        (weights[:, :, None] * out_grad[:, None, :].astype(jnp.float32))
        .astype(jnp.bfloat16)
        .reshape(pair_count, width_part)
    )
    send_grads = jnp.concatenate([pair_grad, zero_row], axis=0)[pair_of_slot].reshape(
        groups, capacity, width_part
    )
    grad_rows = lax.all_to_all(
        send_grads, "expert", split_axis=0, concat_axis=0, tiled=True
    ).reshape(slot_count, width_part)

    def hidden_grad_step(offset, length, current):
        hidden_acc = rounded(contract_last(grad_rows, w_down))
        down_acc = contract_rows(hidden, grad_rows)
        return (hidden_acc, down_acc)

    hidden_grad_part, down_total = run_blocks(
        hidden_grad_step, (zero_hidden, jnp.zeros((hidden_units, width_part), jnp.float32))
    )
    hidden_grad = lax.psum(hidden_grad_part.astype(jnp.bfloat16), "dp").astype(jnp.float32)
    gate_pre_grad, up_pre_grad = swish_grads(hidden_grad, gate_pre, up_pre)

    def token_step(offset, length, current):
        pair_token = (
            contract_last(gate_pre_grad, w_gate) + contract_last(up_pre_grad, w_up)
        ).astype(jnp.bfloat16)
        gate_acc = contract_rows(expert_rows, gate_pre_grad)
        up_acc = contract_rows(expert_rows, up_pre_grad)
        return (pair_token, gate_acc, up_acc)

    zero_weight = jnp.zeros((width_part, hidden_units), jnp.float32)
    token_part, gate_total, up_total = run_blocks(
        token_step, (jnp.zeros((slot_count, width_part), jnp.bfloat16), zero_weight, zero_weight)
    )
    returned_grad = send_back(token_part.reshape(groups, capacity, width_part)).reshape(
        slot_count, width_part
    )
    pair_token_grad = returned_grad[slot_of_pair].reshape(tok_rows, top_count, width_part)
    token_grad = jnp.sum(pair_token_grad.astype(jnp.float32), axis=1).astype(jnp.bfloat16)
    return (
        layer_out,
        token_grad,
        gate_total.astype(jnp.bfloat16)[None],
        up_total.astype(jnp.bfloat16)[None],
        down_total.astype(jnp.bfloat16)[None],
    )


def dense_body(tokens, expert_ids, gate_probs, gate_weight, up_weight, down_weight, out_grad):
    groups = lax.axis_size("expert")
    me = lax.axis_index("expert")
    w_gate = gate_weight[0]
    w_up = up_weight[0]
    w_down = down_weight[0]
    weights = gate_probs / jnp.sum(gate_probs, axis=1, keepdims=True)
    named = expert_ids[:, :, None] == jnp.arange(groups, dtype=jnp.int32)[None, None, :]
    by_expert = jnp.sum(jnp.where(named, weights[:, :, None], 0.0), axis=1)
    all_weights = lax.all_gather(by_expert, "expert", axis=0, tiled=True)
    mine = jnp.arange(groups, dtype=jnp.int32)[None, :] == me
    weight = jnp.sum(jnp.where(mine, all_weights, 0.0), axis=1, keepdims=True)
    rows = lax.all_gather(tokens, "expert", axis=0, tiled=True)
    grads = lax.all_gather(out_grad, "expert", axis=0, tiled=True)
    pair_grad = (weight * grads.astype(jnp.float32)).astype(jnp.bfloat16)

    def total(values):
        return lax.psum(values.astype(jnp.bfloat16), "dp").astype(jnp.float32)

    gate_pre = total(jnp.dot(rows, w_gate, preferred_element_type=jnp.float32))
    up_pre = total(jnp.dot(rows, w_up, preferred_element_type=jnp.float32))
    hidden_grad = total(contract_last(pair_grad, w_down))
    hidden = (jax.nn.silu(gate_pre) * up_pre).astype(jnp.bfloat16)
    expert_out = jnp.dot(hidden, w_down, preferred_element_type=jnp.float32)
    layer_out = lax.psum_scatter(
        (weight * expert_out).astype(jnp.bfloat16), "expert", scatter_dimension=0, tiled=True
    )
    gate_pre_grad, up_pre_grad = swish_grads(hidden_grad, gate_pre, up_pre)
    pair_token = contract_last(gate_pre_grad, w_gate) + contract_last(up_pre_grad, w_up)
    token_grad = lax.psum_scatter(
        pair_token.astype(jnp.bfloat16), "expert", scatter_dimension=0, tiled=True
    )
    return (
        layer_out,
        token_grad,
        contract_rows(rows, gate_pre_grad).astype(jnp.bfloat16)[None],
        contract_rows(rows, up_pre_grad).astype(jnp.bfloat16)[None],
        contract_rows(hidden, pair_grad).astype(jnp.bfloat16)[None],
    )


TILE = 256
BLOCKS = 4
PEERS = 4
MESH = pl.DeviceIdType.MESH


def layer_kernel(
    tok_ref, grad_ref, ids_ref, probs_ref, wg_hbm, wu_hbm, wd_hbm,
    out_ref, tgrad_ref, gg_hbm, ug_hbm, dg_hbm,
    wg_ref, wu_ref, wd_ref, gg_ref, ug_ref, dg_ref,
    tok_all, grd_all, wt_ref, wt_all, wcol, pg_all,
    gu_part, gu_1x, gu_1y, gu_sx, gu_sy, gu_2x, gu_2y,
    hg_part, hg_1x, hg_1y, hg_sx, hg_sy, hg_2x, hg_2y,
    gpre, upre, hid_all, dgu_all,
    eo, eo_in, eo_sum, eo_z, tg, tg_in, tg_sum, tg_z,
    w_s, g_s, d_s,
    tok_s, tok_r, grd_s, grd_r, tokf_s, grdf_s, wt_s, wt_r,
    gu_s, gu_r, hg_s, hg_r, hid_s, hid_r, dgu_s, dgu_r,
    eo_s, eo_r, eoz_s, eoz_r, tg_s, tg_r, tgz_s, tgz_r,
):
    dp = lax.axis_index("dp")
    ex = lax.axis_index("expert")
    z = ex // 2
    c = ex % 2
    oc = 1 - c
    y = dp // 2
    x = dp % 2
    oy = 1 - y
    ox = 1 - x
    dp_x = y * 2 + ox
    dp_y = oy * 2 + x
    rows, width = tok_ref.shape
    units = wg_ref.shape[1]
    share = gu_part.shape[3]
    both = 2 * rows
    bf16 = jnp.bfloat16
    f32 = jnp.float32
    loads = [
        pltpu.make_async_copy(src.at[0], dst, w_s.at[n])
        for n, (src, dst) in enumerate(((wg_hbm, wg_ref), (wu_hbm, wu_ref), (wd_hbm, wd_ref)))
    ]
    for load in loads:
        load.start()

    def block_at(step):
        return ((z // 2 + step // 2) % 2) * 2 + (z + step) % 2

    def remote(src, dst, send, recv, to_dp, to_ex):
        return pltpu.make_async_remote_copy(
            src_ref=src, dst_ref=dst, send_sem=send, recv_sem=recv,
            device_id=(to_dp, to_ex), device_id_type=MESH,
        )

    barrier = pltpu.get_barrier_semaphore()
    for k in range(1, 8):
        pl.semaphore_signal(barrier, inc=1, device_id=(dp, (ex + k) % 8), device_id_type=MESH)
    pl.semaphore_signal(barrier, inc=1, device_id=(dp_x, ex), device_id_type=MESH)
    pl.semaphore_signal(barrier, inc=1, device_id=(dp_y, ex), device_id_type=MESH)

    probs = probs_ref[...]
    weights = probs / jnp.sum(probs, axis=1, keepdims=True)
    lane = lax.broadcasted_iota(jnp.int32, (rows, 128), 1)
    table = jnp.zeros((rows, 128), f32)
    for e in range(8):
        named = jnp.sum(jnp.where(ids_ref[...] == e, weights, 0.0), axis=1, keepdims=True)
        table = jnp.where(lane == e, named, table)
    table = jnp.concatenate([table, jnp.zeros((128 - rows, 128), f32)], axis=0) if rows < 128 else table
    wt_ref[...] = table.T[:8]
    pl.semaphore_wait(barrier, 9)

    def own_copy(src, dst, send, recv, step):
        if step == 0:
            return remote(src, dst.at[z, c], send.at[0], recv.at[z, c], dp, z * 2 + oc)
        return remote(src, dst.at[z, c], send.at[step], recv.at[z, c], dp, block_at(step) * 2 + c)

    def hand_on(dst, send, recv, blk):
        return remote(dst.at[blk, c], dst.at[blk, c], send.at[blk], recv.at[blk, c], dp, z * 2 + oc)

    def arrived(dst, recv, send, blk, core):
        remote(dst.at[blk, core], dst.at[blk, core], send.at[0], recv.at[blk, core], dp, z * 2 + oc).wait_recv()

    inner = jnp.logical_or(z == 1, z == 2)

    def relay(dst, send, recv):
        blk = block_at(2)
        return remote(dst.at[blk, c], dst.at[blk, c], send.at[z], recv.at[blk, c], dp, block_at(1) * 2 + c)

    def send_out(src, dst, send, recv):
        own_copy(src, dst, send, recv, 1).start()
        own_copy(src, dst, send, recv, 2).start()

        @pl.when(inner)
        def _():
            own_copy(src, dst, send, recv, 3).start()

    def grab(dst, send, forward, recv, step):
        blk = block_at(step)
        arrived(dst, recv, send, blk, c)
        if step == 2:
            @pl.when(inner)
            def _():
                relay(dst, forward, recv).start()
        hand_on(dst, forward, recv, blk).start()

    def wt_copy(k):
        return remote(wt_ref, wt_all.at[ex], wt_s.at[k], wt_r.at[ex], dp, (ex + k) % 8)

    own_copy(tok_ref, tok_all, tok_s, tok_r, 0).start()
    for k in range(1, 8):
        wt_copy(k).start()
    send_out(tok_ref, tok_all, tok_s, tok_r)
    tok_all[z, c] = tok_ref[...]
    grd_all[z, c] = grad_ref[...]
    wt_all[ex] = wt_ref[...]
    own_copy(grad_ref, grd_all, grd_s, grd_r, 0).start()

    def first_x(part, into, send, recv, blk):
        half = into.shape[-1]
        return remote(part.at[blk, :, ox, :, pl.ds(0, half)], into.at[blk], send.at[0, blk], recv.at[0, blk], dp_x, ex)

    def first_y(part, into, send, recv, blk):
        half = into.shape[-1]
        return remote(part.at[blk, oy, :, :, pl.ds(half, half)], into.at[blk], send.at[1, blk], recv.at[1, blk], dp_y, ex)

    def second_x(total, into, send, recv, blk):
        return remote(total.at[blk], into.at[blk], send.at[2, blk], recv.at[2, blk], dp_x, ex)

    def second_y(total, into, send, recv, blk):
        return remote(total.at[blk], into.at[blk], send.at[3, blk], recv.at[3, blk], dp_y, ex)

    def pass_on(part, in_x, in_y, sum_x, sum_y, to_x, to_y, send, recv, step):
        blk = block_at(step)
        half = in_x.shape[-1]
        first_x(part, in_x, send, recv, blk).wait_recv()
        sum_y[blk] = (part[blk, oy, x, :, :half].astype(f32) + in_x[blk, oy].astype(f32)).astype(bf16)
        second_y(sum_y, to_y, send, recv, blk).start()
        first_y(part, in_y, send, recv, blk).wait_recv()
        sum_x[blk] = (part[blk, y, ox, :, half:].astype(f32) + in_y[blk, ox].astype(f32)).astype(bf16)
        second_x(sum_x, to_x, send, recv, blk).start()

    def summed(part, in_x, in_y, sum_x, sum_y, to_x, to_y, send, recv, blk):
        half = in_x.shape[-1]
        second_y(sum_y, to_y, send, recv, blk).wait_recv()
        second_x(sum_x, to_x, send, recv, blk).wait_recv()
        low = part[blk, y, x, :, :half].astype(f32) + in_x[blk, y].astype(f32) + to_y[blk].astype(f32)
        high = part[blk, y, x, :, half:].astype(f32) + in_y[blk, x].astype(f32) + to_x[blk].astype(f32)
        return low, high

    def spread(full, send, recv, blk, kind):
        half = full.shape[-1] // 2
        low = pl.ds(0, half)
        high = pl.ds(half, half)
        if kind == 0:
            src, to = full.at[blk, y, x], dp_x
        elif kind == 1:
            src, to = full.at[blk, y, x], dp_y
        elif kind == 2:
            src, to = full.at[blk, oy, x, :, low], dp_x
        else:
            src, to = full.at[blk, y, ox, :, high], dp_y
        return remote(src, src, send.at[kind, blk], recv.at[kind, blk], to, ex)

    def spread_got(full, send, recv, blk, kind):
        half = full.shape[-1] // 2
        if kind == 0:
            dst = full.at[blk, y, ox]
        elif kind == 1:
            dst = full.at[blk, oy, x]
        else:
            dst = full.at[blk, oy, ox, :, pl.ds(0 if kind == 2 else half, half)]
        remote(dst, dst, send.at[kind, blk], recv.at[kind, blk], dp_x, ex).wait_recv()

    def hand_over(full, send, recv, step):
        blk = block_at(step)
        spread_got(full, send, recv, blk, 1)
        spread(full, send, recv, blk, 2).start()
        spread_got(full, send, recv, blk, 0)
        spread(full, send, recv, blk, 3).start()

    def landed(full, send, recv, blk):
        spread_got(full, send, recv, blk, 2)
        spread_got(full, send, recv, blk, 3)

    gu = (gu_part, gu_1x, gu_1y, gu_sx, gu_sy, gu_2x, gu_2y, gu_s, gu_r)
    hg = (hg_part, hg_1x, hg_1y, hg_sx, hg_sy, hg_2x, hg_2y, hg_s, hg_r)

    def gate_up(step):
        blk = block_at(step)
        if step > 0:
            grab(tok_all, tok_s, tokf_s, tok_r, step)
            if step == 1:
                send_out(grad_ref, grd_all, grd_s, grd_r)
        arrived(tok_all, tok_r, tok_s, blk, oc)

        @pl.loop(0, units // TILE)
        def _(j):
            cols = pl.ds(pl.multiple_of(j * TILE, TILE), TILE)
            more = pl.ds(pl.multiple_of(units + j * TILE, TILE), TILE)
            t = tok_all[blk].reshape(both, width)
            gu_part[blk, :, :, :, cols] = jnp.dot(t, wg_ref[:, cols], preferred_element_type=f32).astype(bf16).reshape(2, 2, share, TILE)
            gu_part[blk, :, :, :, more] = jnp.dot(t, wu_ref[:, cols], preferred_element_type=f32).astype(bf16).reshape(2, 2, share, TILE)

        first_x(gu_part, gu_1x, gu_s, gu_r, blk).start()
        first_y(gu_part, gu_1y, gu_s, gu_r, blk).start()

    def hidden_grads(step):
        blk = block_at(step)
        arrived(grd_all, grd_r, grd_s, blk, oc)
        w = wcol[blk].reshape(both, 128)[:, :1]
        pg_all[blk] = (w * grd_all[blk].reshape(both, width).astype(f32)).astype(bf16)

        @pl.loop(0, units // TILE)
        def _(j):
            cols = pl.ds(pl.multiple_of(j * TILE, TILE), TILE)
            part = contract_last(pg_all[blk], wd_ref[cols, :])
            hg_part[blk, :, :, :, cols] = part.astype(bf16).reshape(2, 2, share, TILE)

        first_x(hg_part, hg_1x, hg_s, hg_r, blk).start()
        first_y(hg_part, hg_1y, hg_s, hg_r, blk).start()

    def make_hidden(step):
        blk = block_at(step)
        gate, up = summed(*gu, blk)
        gpre[blk] = gate
        upre[blk] = up
        hid_all[blk, y, x] = (gate * jax.nn.sigmoid(gate) * up).astype(bf16)
        for kind in range(2):
            spread(hid_all, hid_s, hid_r, blk, kind).start()

    def make_grads(step):
        blk = block_at(step)
        hgrad = jnp.concatenate(summed(*hg, blk), axis=1)
        gate = gpre[blk]
        s = jax.nn.sigmoid(gate)
        dgu_all[blk, y, x, :, :units] = (hgrad * upre[blk] * s * (1.0 + gate * (1.0 - s))).astype(bf16)
        dgu_all[blk, y, x, :, units:] = (hgrad * (gate * s)).astype(bf16)
        for kind in range(2):
            spread(dgu_all, dgu_s, dgu_r, blk, kind).start()

    def to_partner(full, into, send, recv, blk):
        return remote(full.at[blk, oc], into.at[blk], send.at[blk], recv.at[blk], dp, z * 2 + oc)

    def home(total, into, send, recv, blk):
        return remote(total.at[blk], into.at[z], send.at[blk], recv.at[z], dp, blk * 2 + c)

    def expert_rows(step):
        blk = block_at(step)
        landed(hid_all, hid_s, hid_r, blk)
        w = wcol[blk].reshape(both, 128)[:, :1]

        @pl.loop(0, width // TILE)
        def _(j):
            cols = pl.ds(pl.multiple_of(j * TILE, TILE), TILE)
            h = hid_all[blk].reshape(both, units)
            part = jnp.dot(h, wd_ref[:, cols], preferred_element_type=f32).astype(bf16)
            eo[blk, :, :, cols] = (w * part.astype(f32)).astype(bf16).reshape(2, rows, TILE)

        to_partner(eo, eo_in, eo_s, eo_r, blk).start()

    def token_rows(step):
        blk = block_at(step)
        landed(dgu_all, dgu_s, dgu_r, blk)

        @pl.loop(0, width // TILE)
        def _(j):
            cols = pl.ds(pl.multiple_of(j * TILE, TILE), TILE)
            part = contract_last(dgu_all[blk, :, :, :, :units].reshape(both, units), wg_ref[cols, :])
            part += contract_last(dgu_all[blk, :, :, :, units:].reshape(both, units), wu_ref[cols, :])
            tg[blk, :, :, cols] = part.astype(bf16).reshape(2, rows, TILE)

        to_partner(tg, tg_in, tg_s, tg_r, blk).start()

    def pair_sum(full, into, total, send, recv, zin, zsend, zrecv, step):
        blk = block_at(step)
        to_partner(full, into, send, recv, blk).wait_recv()
        total[blk] = (full[blk, c].astype(f32) + into[blk].astype(f32)).astype(bf16)
        if step > 0:
            home(total, zin, zsend, zrecv, blk).start()

    def finish(total, zin, zsend, zrecv, result):
        for step in range(1, 4):
            blk = block_at(step)
            remote(total.at[blk], zin.at[blk], zsend.at[blk], zrecv.at[blk], dp, blk * 2 + c).wait_recv()
        zin[z] = total[z]
        result[...] = jnp.sum(zin[...].astype(f32), axis=0).astype(bf16)

    def eo_pair(step):
        pair_sum(eo, eo_in, eo_sum, eo_s, eo_r, eo_z, eoz_s, eoz_r, step)

    def tg_pair(step):
        pair_sum(tg, tg_in, tg_sum, tg_s, tg_r, tg_z, tgz_s, tgz_r, step)

    def hid_over(step):
        hand_over(hid_all, hid_s, hid_r, step)

    def dgu_over(step):
        hand_over(dgu_all, dgu_s, dgu_r, step)

    def grab_grads(step):
        grab(grd_all, grd_s, grdf_s, grd_r, step)

    loads[0].wait()
    loads[1].wait()
    gate_up(0)
    for k in range(1, 8):
        src = (ex + k) % 8
        remote(wt_ref, wt_all.at[src], wt_s.at[k], wt_r.at[src], dp, src).wait_recv()
    diagonal = lax.broadcasted_iota(jnp.int32, (128, 128), 0) == lax.broadcasted_iota(jnp.int32, (128, 128), 1)
    for blk in range(4):
        for core in range(2):
            line = wt_all[blk * 2 + core, pl.ds(ex, 1), :]
            column = jnp.sum(jnp.where(diagonal, line, 0.0), axis=1, keepdims=True)
            wcol[blk, core] = jnp.broadcast_to(column[:rows], (rows, 128))

    loads[2].wait()
    hidden_grads(0)
    gate_up(1)
    pass_on(*gu, 0)
    gate_up(2)
    pass_on(*gu, 1)
    pass_on(*hg, 0)
    gate_up(3)
    pass_on(*gu, 2)
    make_hidden(0)
    grab_grads(2)
    grab_grads(1)
    hidden_grads(1)
    pass_on(*gu, 3)
    hidden_grads(2)
    make_hidden(1)
    pass_on(*hg, 1)
    grab_grads(3)
    hidden_grads(3)
    make_hidden(2)
    pass_on(*hg, 2)
    make_hidden(3)
    hid_over(0)
    hid_over(1)
    pass_on(*hg, 3)
    hid_over(2)
    hid_over(3)
    make_grads(1)
    expert_rows(1)
    make_grads(2)
    expert_rows(2)
    eo_pair(1)
    dgu_over(1)
    make_grads(3)
    expert_rows(3)
    eo_pair(2)
    dgu_over(2)
    make_grads(0)
    eo_pair(3)
    token_rows(1)
    dgu_over(3)
    tg_pair(1)
    token_rows(2)
    dgu_over(0)
    tg_pair(2)
    token_rows(3)
    tg_pair(3)
    expert_rows(0)

    @pl.loop(0, units // TILE)
    def _(j):
        cols = pl.ds(pl.multiple_of(j * TILE, TILE), TILE)
        h = hid_all[:, :, :, :, cols].reshape(BLOCKS * both, TILE)
        dg_ref[cols, :] = contract_rows(h, pg_all[...].reshape(BLOCKS * both, width)).astype(bf16)

    down_store = pltpu.make_async_copy(dg_ref, dg_hbm, d_s)
    down_store.start()
    eo_pair(0)
    token_rows(0)

    def stores(j):
        cols = pl.ds(pl.multiple_of(j * TILE, TILE), TILE)
        return (
            pltpu.make_async_copy(gg_ref.at[cols, :], gg_hbm.at[cols, :], g_s.at[0, j]),
            pltpu.make_async_copy(ug_ref.at[cols, :], ug_hbm.at[cols, :], g_s.at[1, j]),
        )

    @pl.loop(0, width // TILE)
    def _(j):
        cols = pl.ds(pl.multiple_of(j * TILE, TILE), TILE)
        t = tok_all[:, :, :, cols].reshape(BLOCKS * both, TILE)
        gg_ref[cols, :] = contract_rows(t, dgu_all[:, :, :, :, :units].reshape(BLOCKS * both, units)).astype(bf16)
        ug_ref[cols, :] = contract_rows(t, dgu_all[:, :, :, :, units:].reshape(BLOCKS * both, units)).astype(bf16)
        for store in stores(j):
            store.start()

    tg_pair(0)
    finish(eo_sum, eo_z, eoz_s, eoz_r, out_ref)
    finish(tg_sum, tg_z, tgz_s, tgz_r, tgrad_ref)

    for step in range(4):
        blk = block_at(step)
        if step < 3:
            own_copy(tok_ref, tok_all, tok_s, tok_r, step).wait_send()
            own_copy(grad_ref, grd_all, grd_s, grd_r, step).wait_send()
        if step > 0:
            hand_on(tok_all, tokf_s, tok_r, blk).wait_send()
            hand_on(grd_all, grdf_s, grd_r, blk).wait_send()
            home(eo_sum, eo_z, eoz_s, eoz_r, blk).wait_send()
            home(tg_sum, tg_z, tgz_s, tgz_r, blk).wait_send()
        to_partner(eo, eo_in, eo_s, eo_r, blk).wait_send()
        to_partner(tg, tg_in, tg_s, tg_r, blk).wait_send()
        for part, in_x, in_y, sum_x, sum_y, to_x, to_y, send, recv in (gu, hg):
            first_x(part, in_x, send, recv, blk).wait_send()
            first_y(part, in_y, send, recv, blk).wait_send()
            second_x(sum_x, to_x, send, recv, blk).wait_send()
            second_y(sum_y, to_y, send, recv, blk).wait_send()
        for kind in range(4):
            spread(hid_all, hid_s, hid_r, blk, kind).wait_send()
            spread(dgu_all, dgu_s, dgu_r, blk, kind).wait_send()
    for k in range(1, 8):
        wt_copy(k).wait_send()
    down_store.wait()

    @pl.when(inner)
    def _():
        own_copy(tok_ref, tok_all, tok_s, tok_r, 3).wait_send()
        own_copy(grad_ref, grd_all, grd_s, grd_r, 3).wait_send()
        relay(tok_all, tokf_s, tok_r).wait_send()
        relay(grd_all, grdf_s, grd_r).wait_send()

    @pl.loop(0, width // TILE)
    def _(j):
        for store in stores(j):
            store.wait()


def kernel_body(tokens, expert_ids, gate_probs, gate_weight, up_weight, down_weight, out_grad):
    rows, width = tokens.shape
    units = gate_weight.shape[2]
    share = 2 * rows // PEERS
    bf16 = jnp.bfloat16
    f32 = jnp.float32

    def vm(*shape, dtype=bf16):
        return pltpu.VMEM(shape, dtype)

    def sem(*shape):
        return pltpu.SemaphoreType.DMA(shape)

    whole = pl.BlockSpec(memory_space=pltpu.VMEM)
    shapes = [(rows, width), (rows, width), (width, units), (width, units), (units, width)]
    flops = 2 * 9 * 8 * rows * width * units
    anywhere = pl.BlockSpec(memory_space=pl.ANY)

    def exchange(columns):
        half = columns // 2
        return [vm(4, 2, 2, share, columns), vm(4, 2, share, half), vm(4, 2, share, half)] + [
            vm(4, share, half)
        ] * 4

    results = pl.pallas_call(
        layer_kernel,
        out_shape=[jax.ShapeDtypeStruct(shape, bf16) for shape in shapes],
        in_specs=[whole] * 4 + [anywhere] * 3,
        out_specs=[whole] * 2 + [anywhere] * 3,
        scratch_shapes=[
            vm(width, units), vm(width, units), vm(units, width),
            vm(width, units), vm(width, units), vm(units, width),
            vm(4, 2, rows, width), vm(4, 2, rows, width), vm(8, 128, dtype=f32), vm(8, 8, 128, dtype=f32),
            vm(4, 2, rows, 128, dtype=f32), vm(4, 2 * rows, width),
            *exchange(2 * units), *exchange(units),
            vm(4, share, units, dtype=f32), vm(4, share, units, dtype=f32),
            vm(4, 2, 2, share, units), vm(4, 2, 2, share, 2 * units),
            vm(4, 2, rows, width), vm(4, rows, width), vm(4, rows, width), vm(4, rows, width),
            vm(4, 2, rows, width), vm(4, rows, width), vm(4, rows, width), vm(4, rows, width),
            sem(3), sem(2, width // TILE), pltpu.SemaphoreType.DMA,
            sem(4), sem(4, 2), sem(4), sem(4, 2), sem(4), sem(4), sem(8), sem(8),
            sem(4, 4), sem(4, 4), sem(4, 4), sem(4, 4), sem(4, 4), sem(4, 4), sem(4, 4), sem(4, 4),
            sem(4), sem(4), sem(4), sem(4), sem(4), sem(4), sem(4), sem(4),
        ],
        compiler_params=pltpu.CompilerParams(
            collective_id=0, has_side_effects=True, vmem_limit_bytes=48 * 1024 * 1024
        ),
        cost_estimate=pl.CostEstimate(flops=flops, bytes_accessed=12_000_000, transcendentals=0),
        name="moe_layer",
    )(tokens, out_grad, expert_ids, gate_probs, gate_weight, up_weight, down_weight)
    layer_out, token_grad, gate_grad, up_grad, down_grad = results
    return layer_out, token_grad, gate_grad[None], up_grad[None], down_grad[None]


def body(tokens, expert_ids, *rest):
    groups = lax.axis_size("expert")
    if expert_ids.shape[1] == groups:
        fits = tokens.shape[0] % 32 == 0 and tokens.shape[0] <= 128
        if groups == 8 and lax.axis_size("dp") == 4 and fits:
            return kernel_body(tokens, expert_ids, *rest)
        return dense_body(tokens, expert_ids, *rest)
    return sparse_body(tokens, expert_ids, *rest)


def solution(mesh):
    placed = (
        P("expert", "dp"),
        P("expert", None),
        P("expert", None),
        P("expert", "dp", None),
        P("expert", "dp", None),
        P("expert", None, "dp"),
        P("expert", "dp"),
    )
    return jax.shard_map(
        body,
        mesh=mesh,
        in_specs=placed,
        out_specs=(
            P("expert", "dp"),
            P("expert", "dp"),
            P("expert", "dp", None),
            P("expert", "dp", None),
            P("expert", None, "dp"),
        ),
        check_vma=False,
    )
```
